128 devices in a mesh: seq: 16 (over z, x), tensor: 8 (over y, core).
Axes of the slice: x: 4, y: 4, z: 4, core: 2. Of those that a mesh axis runs over, the one named last changes fastest.
Arguments:
- queries: bfloat16 [4096, 4096], P('seq', 'tensor'), may hold values from -20 to 20
- out_grad: bfloat16 [4096, 4096], P('seq', 'tensor'), may hold values from -6 to 6
- neighbours: bfloat16 [18432, 4096], P('seq', 'tensor'), may hold values from -6 to 6
- key_weight: bfloat16 [4096, 4096], P(None, 'tensor'), may hold values from -0.09375 to 0.09375
- value_weight: bfloat16 [4096, 4096], P(None, 'tensor'), may hold values from -0.09375 to 0.09375
- owner: int32 [64, 2], replicated, may hold values from 0 to 15, as said below
- slot: int32 [64, 2], replicated, may hold values from 0 to 8, as said below
- lengths: int32 [16, 9], replicated, may hold values from 8 to 128, as said below
Outputs:
- query_grad: bfloat16 [4096, 4096], P('seq', 'tensor')
- key_weight_grad: float32 [4096, 4096], P('seq', 'tensor')
- value_weight_grad: float32 [4096, 4096], P('seq', 'tensor')
- neighbour_grad: bfloat16 [18432, 4096], P('seq', 'tensor')
The draws below stay inside these ranges and needn't reach their ends.
Inputs may be any that keep to these rules, and one draw needn't show every extreme that they name: Each (owner, slot) pair is named by exactly one block's neighbour; the slots named on one shard are 0 to its count of neighbours minus 1; a shard holds at most 9 neighbours, and at least half of the shards hold exactly 9. The 8 neighbours of the blocks of one seq index come at most 1 from one shard. `slot`: see owner. `lengths`: every encoder shard has some neighbour with all 128 rows valid.
All inputs are finite; a program needn't handle non-finite values.
Results may differ from the reference program's by a relative error of at most 0.02.
The reference program's roundings to bfloat16 on the way (of `attention_low`, `value_grad`, `score_grad` and `key_grad`) count: a program that leaves them out, or rounds other values in their place, can miss the bound.
Values may be sent and summed in bfloat16 or wider, within the bound.
No kernel may reach another device: no remote copies, remote signals or barrier semaphores. Data moves between devices by JAX's collectives and lax.ppermute only.
A program may use at most 128 MiB of HBM per device.

```python
import jax
import jax.numpy as jnp
from jax import lax

D = 4096
HEAD = 128
BLOCK = 64
NEIGHBOUR_TOKENS = 128
NEIGH = 2
REFS = 8
SHARD_SLOTS = 9
TOKENS = 4096
BLOCKS = 64
SLOTS = 144
ENC_ROWS = 18432
N_SEQ = 16
N_TENSOR = 8


def routing_tables(key):
    shard_count = N_SEQ
    order_key, reader_key, shuffle_key, rank_key = jax.random.split(key, 4)
    order = jax.random.permutation(order_key, shard_count).astype(jnp.int32)
    readers = jax.random.permutation(reader_key, shard_count).astype(jnp.int32)
    places = jnp.arange(shard_count, dtype=jnp.int32)
    design = (places[:, None] + jnp.arange(REFS, dtype=jnp.int32)[None, :]) % shard_count
    if shard_count > REFS:
        moved = jnp.where(places % 2 == 1, places - 1, places)
        design = design.at[:, 0].set(moved)
    design = jnp.take(design, readers, axis=0)
    holders = jnp.take(order, design)
    shuffles = jax.vmap(lambda subkey: jax.random.permutation(subkey, REFS))(jax.random.split(shuffle_key, shard_count))
    holders = jnp.take_along_axis(holders, shuffles.astype(jnp.int32), axis=1).reshape(-1)
    priority = jax.random.permutation(rank_key, REFS * shard_count)
    same_holder = holders[:, None] == holders[None, :]
    before = priority[None, :] < priority[:, None]
    slots = jnp.sum(same_holder & before, axis=1).astype(jnp.int32)
    return (holders.reshape(BLOCKS, NEIGH), slots.reshape(BLOCKS, NEIGH))


def draw_owner(key, part):
    tables = routing_tables(key)
    return tables[0]


def draw_slot(key, part):
    tables = routing_tables(key)
    return tables[1]


def draw_lengths(key, part):
    key = jax.random.fold_in(key, 3)
    root_random_key, pick_key = jax.random.split(key)
    base_offset = jax.random.randint(root_random_key, (N_SEQ, SHARD_SLOTS), 8, NEIGHBOUR_TOKENS + 1)
    chosen = jax.random.randint(pick_key, (N_SEQ, 1), 0, 2)
    column_indices = jnp.arange(SHARD_SLOTS, dtype=jnp.int32)[None, :]
    return jnp.where(column_indices == chosen, NEIGHBOUR_TOKENS, base_offset).astype(jnp.int32)


def draw_queries(key, part):
    key = jax.random.fold_in(key, 5)
    second_key = jax.random.fold_in(key, 1)
    values_out = jnp.clip(jax.random.normal(second_key, (TOKENS, D)), -4.0, 4.0)
    return values_out.astype(jnp.bfloat16)


def shard_levels(key, extent, cuts, smallest, high):
    level, own = 1.0, jax.random.fold_in(key, 6)
    for position, parts in cuts:
        draws = jnp.exp(jax.random.uniform(jax.random.fold_in(own, position), (parts,), jnp.float32, smallest / len(cuts), high / len(cuts)))
        level = level * jnp.repeat(draws, extent[position] // parts).reshape([-1 if axis == position else 1 for axis in range(len(extent))])
    return level


def centred(key, shape, scale, limit, cuts=(), kind=jnp.bfloat16):
    values = jax.random.normal(key, shape, jnp.float32) * scale
    if len(cuts) > 0:
        values = shard_levels(key, shape, cuts, -0.22, 0.18) * values
    return jnp.clip(values, min=-limit, max=limit).astype(kind)


def setup_inputs(seed: int = 0) -> dict:
    arg_keys = jax.random.split(jax.random.key(seed), 9)
    return {
        "queries": draw_queries(jax.random.fold_in(arg_keys[8], 71), 0),
        "out_grad": centred(arg_keys[1], (TOKENS, D), 1.0, 6.0, ((0, 16), (1, 8))),
        "neighbours": centred(arg_keys[2], (ENC_ROWS, D), 1.0, 6.0, ((0, 16), (1, 8))),
        "key_weight": centred(arg_keys[3], (D, D), D ** -0.5, 0.09375, ((1, 8),)),
        "value_weight": centred(arg_keys[4], (D, D), D ** -0.5, 0.09375, ((1, 8),)),
        "owner": draw_owner(jax.random.fold_in(arg_keys[8], 71), 0),
        "slot": draw_slot(jax.random.fold_in(arg_keys[8], 71), 0),
        "lengths": draw_lengths(jax.random.fold_in(arg_keys[8], 71), 0),
    }


def rounded(values_in):
    return lax.optimization_barrier(values_in.astype(jnp.bfloat16)).astype(jnp.float32)


def attend_back(queries, out_grad, key_rows, value_rows, valid_lengths):
    tokens, width = queries.shape
    blocks = tokens // BLOCK
    heads = width // HEAD
    span = NEIGH * NEIGHBOUR_TOKENS
    scale = HEAD ** -0.5
    query_heads = queries.astype(jnp.float32).reshape(blocks, BLOCK, heads, HEAD)
    grad_heads = out_grad.astype(jnp.float32).reshape(blocks, BLOCK, heads, HEAD)
    key_heads = key_rows.astype(jnp.float32).reshape(blocks, span, heads, HEAD)
    value_heads = value_rows.astype(jnp.float32).reshape(blocks, span, heads, HEAD)
    valid_keys = (jnp.arange(NEIGHBOUR_TOKENS, dtype=jnp.int32)[None, :] < valid_lengths[:, None]).reshape(blocks, span)
    scores = jnp.einsum("cqhd,ckhd->chqk", query_heads, key_heads) * scale
    scores = jnp.where(valid_keys[:, None, None, :], scores, -jnp.inf)
    highest = jnp.max(scores, axis=-1, keepdims=True)
    raised = jnp.exp(scores - highest)
    attention = raised / jnp.sum(raised, axis=-1, keepdims=True)
    attention_low = rounded(attention)
    attended = jnp.einsum("chqk,ckhd->cqhd", attention_low, value_heads)
    delta = jnp.sum(attended * grad_heads, axis=-1).transpose(0, 2, 1)[..., None]
    value_grad = jnp.einsum("chqk,cqhd->ckhd", attention_low, grad_heads).astype(jnp.bfloat16)
    prob_grad = jnp.einsum("cqhd,ckhd->chqk", grad_heads, value_heads)
    score_grad = rounded(attention * (prob_grad - delta) * scale)
    query_grad = jnp.einsum("chqk,ckhd->cqhd", score_grad, key_heads).astype(jnp.bfloat16)
    key_grad = jnp.einsum("chqk,cqhd->ckhd", score_grad, query_heads).astype(jnp.bfloat16)
    refs = blocks * NEIGH
    return (query_grad.reshape(tokens, width), key_grad.reshape(refs, NEIGHBOUR_TOKENS, width), value_grad.reshape(refs, NEIGHBOUR_TOKENS, width))


def reference(queries, out_grad, neighbours, key_weight, value_weight, owner, slot, lengths):
    flattened_rows = (owner * SHARD_SLOTS + slot).reshape(-1).astype(jnp.int32)
    slot_rows = neighbours.reshape(SLOTS, NEIGHBOUR_TOKENS, D)
    picked = jnp.take(slot_rows, flattened_rows, axis=0).reshape(-1, D)
    key_rows = jnp.dot(picked, key_weight, preferred_element_type=jnp.float32).astype(jnp.bfloat16)
    value_rows = jnp.dot(picked, value_weight, preferred_element_type=jnp.float32).astype(jnp.bfloat16)
    valid_lengths = jnp.take(lengths.reshape(-1), flattened_rows)
    query_grad, key_grad, value_grad = attend_back(queries, out_grad, key_rows, value_rows, valid_lengths)
    pair = jnp.concatenate([key_grad, value_grad], axis=-1)
    slot_grads = jnp.zeros((SLOTS, NEIGHBOUR_TOKENS, 2 * D), jnp.bfloat16).at[flattened_rows].set(pair).reshape(ENC_ROWS, 2 * D)
    rows_per_shard = SHARD_SLOTS * NEIGHBOUR_TOKENS

    def weight_step(total, index):
        rows_here = lax.dynamic_slice_in_dim(neighbours, index * rows_per_shard, rows_per_shard, 0)
        grads_here = lax.dynamic_slice_in_dim(slot_grads, index * rows_per_shard, rows_per_shard, 0)
        term = jnp.dot(rows_here.T, grads_here, preferred_element_type=jnp.float32)
        return total + rounded(term), None

    weight_total, _ = lax.scan(weight_step, jnp.zeros((D, 2 * D), jnp.float32), jnp.arange(N_SEQ, dtype=jnp.int32))
    read_grads = pair.reshape(-1, 2 * D)
    width = D // N_TENSOR
    dims = (((1,), (1,)), ((), ()))

    def feature_step(total, index):
        start = index * width
        key_part = lax.dynamic_slice_in_dim(read_grads, start, width, 1)
        value_part = lax.dynamic_slice_in_dim(read_grads, D + start, width, 1)
        key_cols = lax.dynamic_slice_in_dim(key_weight, start, width, 1)
        value_cols = lax.dynamic_slice_in_dim(value_weight, start, width, 1)
        term = lax.dot_general(key_part, key_cols, dims, preferred_element_type=jnp.float32)
        term = term + lax.dot_general(value_part, value_cols, dims, preferred_element_type=jnp.float32)
        return total + rounded(term), None

    feature_total, _ = lax.scan(feature_step, jnp.zeros((read_grads.shape[0], D), jnp.float32), jnp.arange(N_TENSOR, dtype=jnp.int32))
    read_rows = feature_total.astype(jnp.bfloat16).reshape(-1, NEIGHBOUR_TOKENS, D)
    neighbour_grad = jnp.zeros((SLOTS, NEIGHBOUR_TOKENS, D), jnp.bfloat16).at[flattened_rows].set(read_rows).reshape(ENC_ROWS, D)
    return (query_grad, weight_total[:, :D], weight_total[:, D:], neighbour_grad)
```

```python
import jax
import jax.numpy as jnp
from jax import lax
from jax.experimental import pallas as pl
from jax.experimental.pallas import tpu as pltpu
from jax.sharding import PartitionSpec as P

HEAD = 128
BLOCK = 64
NT = 128
NEIGH = 2
VMEM_LIMIT = 48 * 1024 * 1024
F32 = jnp.float32
BF16 = jnp.bfloat16


def params():
    return pltpu.CompilerParams(vmem_limit_bytes=VMEM_LIMIT)


def cost(flops, moved):
    return pl.CostEstimate(flops=flops, bytes_accessed=moved, transcendentals=0)


def dot(a, b, ca, cb):
    return lax.dot_general(a, b, (((ca,), (cb,)), ((), ())), preferred_element_type=F32)


def project(rows, key_weight, value_weight):
    parts, count, depth = rows.shape
    width = key_weight.shape[1]

    def body(r_ref, k_ref, v_ref, o_ref, acc):
        step = pl.program_id(0)

        @pl.when(step == 0)
        def _():
            acc[...] = jnp.zeros_like(acc)

        acc[:, :width] += dot(r_ref[0], k_ref[...], 1, 0)
        acc[:, width:] += dot(r_ref[0], v_ref[...], 1, 0)

        @pl.when(step == parts - 1)
        def _():
            o_ref[...] = acc[...].astype(BF16)

    return pl.pallas_call(
        body,
        grid=(parts,),
        in_specs=[
            pl.BlockSpec((1, count, depth), lambda i: (i, 0, 0)),
            pl.BlockSpec((depth, width), lambda i: (i, 0)),
            pl.BlockSpec((depth, width), lambda i: (i, 0)),
        ],
        out_specs=pl.BlockSpec((count, 2 * width), lambda i: (0, 0)),
        out_shape=jax.ShapeDtypeStruct((count, 2 * width), BF16),
        scratch_shapes=[pltpu.VMEM((count, 2 * width), F32)],
        compiler_params=params(),
        cost_estimate=cost(4 * parts * count * depth * width, 20 << 20),
        name="project",
    )(rows, key_weight, value_weight)


def attend_back(queries, out_grad, pair_rows, lengths):
    tokens, width = queries.shape
    blocks = tokens // BLOCK
    heads = width // HEAD
    span = NEIGH * NT
    scale = HEAD ** (-0.5)

    def body(len_ref, q_ref, g_ref, kv_ref, dq_ref, p_ref, t_ref):
        block = pl.program_id(0)
        column = lax.broadcasted_iota(jnp.int32, (BLOCK, span), 1)
        first = len_ref[block * NEIGH]
        second = len_ref[block * NEIGH + 1]
        valid = (column < first) | ((column >= NT) & (column < NT + second))
        for h in range(heads):
            cols = slice(h * HEAD, (h + 1) * HEAD)
            vcols = slice(width + h * HEAD, width + (h + 1) * HEAD)
            q = q_ref[:, cols]
            g = g_ref[:, cols]
            k = kv_ref[:, cols]
            v = kv_ref[:, vcols]
            scores = jnp.where(valid, dot(q, k, 1, 1) * scale, -jnp.inf)
            raised = jnp.exp(scores - jnp.max(scores, axis=1, keepdims=True))
            attention = raised / jnp.sum(raised, axis=1, keepdims=True)
            low = attention.astype(BF16)
            prob_grad = dot(g, v, 1, 1)
            delta = jnp.sum(low.astype(F32) * prob_grad, axis=1, keepdims=True)
            score_grad = (attention * (prob_grad - delta) * scale).astype(BF16)
            dq_ref[:, cols] = dot(score_grad, k, 1, 0).astype(BF16)
            p_ref[:, cols] = dot(score_grad, q, 0, 0).astype(BF16)
            p_ref[:, vcols] = dot(low, g, 0, 0).astype(BF16)
            t_ref[cols, :] = dot(q, score_grad, 0, 0).astype(BF16)
            t_ref[vcols, :] = dot(g, low, 0, 0).astype(BF16)

    count = blocks * span
    return pl.pallas_call(
        body,
        grid_spec=pltpu.PrefetchScalarGridSpec(
            num_scalar_prefetch=1,
            grid=(blocks,),
            in_specs=[
                pl.BlockSpec((BLOCK, width), lambda i, n: (i, 0)),
                pl.BlockSpec((BLOCK, width), lambda i, n: (i, 0)),
                pl.BlockSpec((span, 2 * width), lambda i, n: (i, 0)),
            ],
            out_specs=[
                pl.BlockSpec((BLOCK, width), lambda i, n: (i, 0)),
                pl.BlockSpec((span, 2 * width), lambda i, n: (i, 0)),
                pl.BlockSpec((2 * width, span), lambda i, n: (0, i)),
            ],
        ),
        out_shape=[
            jax.ShapeDtypeStruct((tokens, width), BF16),
            jax.ShapeDtypeStruct((count, 2 * width), BF16),
            jax.ShapeDtypeStruct((2 * width, count), BF16),
        ],
        compiler_params=params(),
        cost_estimate=cost(7 * 2 * tokens * span * width, 8 << 20),
        name="attend_back",
    )(lengths, queries, out_grad, pair_rows)


def weight_groups(grads_t, rows, groups, split):
    width, count = grads_t.shape[0] // 2, grads_t.shape[1]
    chunk = 256
    total = len(groups) * split
    halves = [g[0] for g in groups]
    ids = jnp.stack([jnp.stack(g[1] + g[2]) for g in groups]).reshape(-1).astype(jnp.int32)

    def body(id_ref, *refs):
        t_refs, r_refs, o_refs = refs[:2], refs[2 : 2 + len(groups)], refs[2 + len(groups) :]
        for half, r_ref, o_ref in zip(halves, r_refs, o_refs):
            o_ref[0] = dot(t_refs[half][...], r_ref[0], 1, 0).astype(BF16)

    def row_spec(n):
        base = n * 2 * split
        return pl.BlockSpec((1, count, chunk), lambda i, s: (s[base + i], 0, s[base + split + i]))

    return pl.pallas_call(
        body,
        grid_spec=pltpu.PrefetchScalarGridSpec(
            num_scalar_prefetch=1,
            grid=(split,),
            in_specs=[
                pl.BlockSpec((width, count), lambda i, s: (0, 0)),
                pl.BlockSpec((width, count), lambda i, s: (1, 0)),
            ]
            + [row_spec(n) for n in range(len(groups))],
            out_specs=[pl.BlockSpec((1, width, chunk), lambda i, s: (i, 0, 0)) for _ in groups],
        ),
        out_shape=[jax.ShapeDtypeStruct((split, width, chunk), BF16) for _ in groups],
        compiler_params=params(),
        cost_estimate=cost(2 * total * width * count * chunk, total * 3 << 18),
        name="weight_groups",
    )(ids, grads_t, grads_t, *([rows] * len(groups)))


def row_part(pair, key_weight, value_weight):
    count = pair.shape[0]
    features, width = key_weight.shape
    tile = 512

    def body(p_ref, k_ref, v_ref, o_ref):
        term = dot(p_ref[:, :width], k_ref[...], 1, 1)
        o_ref[...] = (term + dot(p_ref[:, width:], v_ref[...], 1, 1)).astype(BF16)

    return pl.pallas_call(
        body,
        grid=(features // tile,),
        in_specs=[
            pl.BlockSpec((count, 2 * width), lambda i: (0, 0)),
            pl.BlockSpec((tile, width), lambda i: (i, 0)),
            pl.BlockSpec((tile, width), lambda i: (i, 0)),
        ],
        out_specs=pl.BlockSpec((count, tile), lambda i: (0, i)),
        out_shape=jax.ShapeDtypeStruct((count, features), BF16),
        compiler_params=params(),
        cost_estimate=cost(4 * count * features * width, 18 << 20),
        name="row_part",
    )(pair, key_weight, value_weight)


def shift(value, axis, step):
    def moved(i):
        z, x = i // 4, i % 4
        return ((z + step) % 4) * 4 + x if axis == "z" else z * 4 + (x + step) % 4

    return lax.ppermute(value, "seq", [(i, moved(i)) for i in range(16)])


def add(*terms):
    total = terms[0].astype(F32)
    for term in terms[1:]:
        total = total + term.astype(F32)
    return total.astype(BF16)


def ring_first(axis, far_lo, far_hi, next_lo, next_hi, last_lo, last_hi):
    via_up = shift(far_lo, axis, 1)
    via_down = shift(far_hi, axis, -1)
    up_hi = shift(next_hi, axis, 1)
    down_lo = shift(last_lo, axis, -1)
    up_lo = shift(add(next_lo, via_up), axis, 1)
    down_hi = shift(add(last_hi, via_down), axis, -1)
    return (up_lo, down_lo), (up_hi, down_hi)


def weight_grads(grads_t, rows):
    spot = lax.axis_index("seq")
    z, x = spot // 4, spot % 4

    def key_group(step, pick):
        col = (x + step) % 4
        return (0, [2 * ((z + d) % 4) + col // 2 for d in pick], [col % 2 for _ in pick])

    def value_group(step, pick):
        return (
            1,
            [2 * ((z + step) % 4) + ((x + d) % 4) // 2 for d in pick],
            [((x + d) % 4) % 2 for d in pick],
        )

    lo, hi = (0, 1), (2, 3)
    k2l, k2h, v2l, v2h = weight_groups(
        grads_t, rows, [key_group(2, lo), key_group(2, hi), value_group(2, lo), value_group(2, hi)], 2
    )
    k1l, k1h, k3l, k3h, v1l, v1h, v3l, v3h = weight_groups(
        grads_t,
        rows,
        [
            key_group(1, lo), key_group(1, hi), key_group(3, lo), key_group(3, hi),
            value_group(1, lo), value_group(1, hi), value_group(3, lo), value_group(3, hi),
        ],
        2,
    )
    own = weight_groups(
        grads_t, rows, [key_group(0, lo), key_group(0, hi), value_group(0, lo), value_group(0, hi)], 2
    )
    key_lo, key_hi = ring_first("x", k2l, k2h, k1l, k1h, k3l, k3h)
    value_lo, value_hi = ring_first("z", v2l, v2h, v1l, v1h, v3l, v3h)
    done = []
    for axis, o_lo, o_hi, (a, b), (c, d) in (
        ("z", own[0], own[1], key_lo, key_hi),
        ("x", own[2], own[3], value_lo, value_hi),
    ):
        half = o_lo.shape[1] // 2
        far = add(o_hi[0], c[0], d[0])
        after = add(o_lo[1], a[1], b[1])
        before = add(o_hi[1], c[1], d[1])
        via_up = shift(far[:half], axis, 1)
        via_down = shift(far[half:], axis, -1)
        up_hi = shift(after[half:], axis, 1)
        down_lo = shift(before[:half], axis, -1)
        up_lo = shift(add(after[:half], via_up), axis, 1)
        down_hi = shift(add(before[half:], via_down), axis, -1)
        mine = o_lo[0].astype(F32) + a[0].astype(F32) + b[0].astype(F32)
        low = mine[:half] + up_lo.astype(F32) + down_lo.astype(F32)
        high = mine[half:] + up_hi.astype(F32) + down_hi.astype(F32)
        done.append(jnp.concatenate([low, high], axis=0).T)
    return done


def local(queries, out_grad, neighbours, key_weight, value_weight, owner, slot, lengths):
    seq_count = lax.axis_size("seq")
    position = lax.axis_index("seq")
    slot_count = lengths.shape[1]
    width = key_weight.shape[1]
    holders = owner.reshape(seq_count, -1)
    slots = slot.reshape(seq_count, -1)
    refs = holders.shape[1]
    order = jnp.arange(refs, dtype=jnp.int32)
    readers = jnp.arange(seq_count, dtype=jnp.int32)

    mine = holders == position
    send_slot = jnp.sum(jnp.where(mine, slots, 0), axis=1)
    my_holder = lax.dynamic_index_in_dim(holders, position, 0, keepdims=False)
    my_slot = lax.dynamic_index_in_dim(slots, position, 0, keepdims=False)
    my_lengths = jnp.take(lengths.reshape(-1), my_holder * slot_count + my_slot, mode="clip")
    back_ref = jnp.sum(jnp.where(my_holder[:, None] == readers[None, :], order[:, None], 0), axis=0)
    reads = mine[:, :, None] & (slots[:, :, None] == jnp.arange(slot_count, dtype=jnp.int32))
    slot_reader = jnp.sum(jnp.where(reads, readers[:, None, None], 0), axis=(0, 1))
    slot_live = jnp.any(reads, axis=(0, 1))

    outgoing = jnp.take(neighbours.reshape(slot_count, NT, width), send_slot, axis=0, mode="clip")
    incoming = lax.all_to_all(outgoing, "seq", split_axis=0, concat_axis=0, tiled=True)
    read = jnp.take(incoming, my_holder, axis=0, mode="clip").reshape(refs * NT, width)
    rows = lax.all_gather(read, "tensor", axis=0, tiled=False)
    pair_rows = project(rows, key_weight, value_weight)
    query_grad, pair, pair_t = attend_back(queries, out_grad, pair_rows, my_lengths)
    part = row_part(pair, key_weight, value_weight)
    row_grad = lax.psum_scatter(part, "tensor", scatter_dimension=1, tiled=True)
    key_weight_grad, value_weight_grad = weight_grads(pair_t, rows)
    returning = jnp.take(row_grad.reshape(refs, NT, width), back_ref, axis=0, mode="clip")
    arrived = lax.all_to_all(returning, "seq", split_axis=0, concat_axis=0, tiled=True)
    taken = jnp.take(arrived, slot_reader, axis=0, mode="clip")
    neighbour_grad = jnp.where(slot_live[:, None, None], taken, jnp.zeros((), BF16))
    return (
        query_grad,
        key_weight_grad,
        value_weight_grad,
        neighbour_grad.reshape(slot_count * NT, width),
    )


def solution(mesh):
    placed = (
        P("seq", "tensor"),
        P("seq", "tensor"),
        P("seq", "tensor"),
        P(None, "tensor"),
        P(None, "tensor"),
        P(),
        P(),
        P(),
    )
    return jax.shard_map(
        local,
        mesh=mesh,
        in_specs=placed,
        out_specs=(P("seq", "tensor"), P("seq", "tensor"), P("seq", "tensor"), P("seq", "tensor")),
        check_vma=False,
    )
```

```python
import jax
import jax.numpy as jnp
from jax import lax
from jax.experimental import pallas as pl
from jax.experimental.pallas import tpu as pltpu
from jax.sharding import PartitionSpec as P

HEAD = 128
BLOCK = 64
NT = 128
NEIGH = 2
VMEM_LIMIT = 60 * 1024 * 1024
F32 = jnp.float32
BF16 = jnp.bfloat16


def params():
    return pltpu.CompilerParams(vmem_limit_bytes=VMEM_LIMIT)


def cost(flops, moved):
    return pl.CostEstimate(flops=flops // 1024, bytes_accessed=moved // 1024, transcendentals=0)


def dot(a, b, ca, cb):
    return lax.dot_general(a, b, (((ca,), (cb,)), ((), ())), preferred_element_type=F32)


ANY = pl.BlockSpec(memory_space=pl.ANY)
VMEM = pl.BlockSpec(memory_space=pltpu.VMEM)
SMEM = pl.BlockSpec(memory_space=pltpu.SMEM)


FAR, BACK, ON, OWN = 0, 1, 2, 3


def here():
    spot, column = lax.axis_index("seq"), lax.axis_index("tensor")
    return spot >> 2, spot & 3, column >> 1, column & 1


def moved(at, step):
    way = 1 - 2 * here()[3]
    return (at + (2, -way, way, 0)[step]) & 3


def piece_block(n):
    core = here()[3]
    step, other = ((OWN, 0), (OWN, 1), (BACK, 0), (ON, 1), (ON, 0), (BACK, 1), (FAR, 0), (FAR, 1))[n]
    return 2 * moved(here()[2], step) + (core ^ other)


def chunk_place(z, x):
    _, _, y, core = here()
    step, other = (z - y) & 3, (x >> 1) ^ core
    behind = step == moved(0, BACK)
    piece = jnp.where(
        step == 0,
        other,
        jnp.where(step == 2, 6 + other, jnp.where(behind, jnp.where(other == 1, 5, 2), jnp.where(other == 1, 3, 4))),
    )
    return 2 * piece + (x & 1)


def chunk_places(kind, step):
    z, x, _, _ = here()
    if kind == 0:
        return [chunk_place(moved(z, n), moved(x, step)) for n in range(4)]
    return [chunk_place(moved(z, step), moved(x, n)) for n in range(4)]


def spread(neighbours, send_slot, half):
    slots, rows, width = neighbours.shape
    count, part = send_slot.shape[0], rows // 2

    def body(s_ref, n_ref, o_ref, sems):
        copies = [
            pltpu.make_async_copy(
                n_ref.at[s_ref[p], pl.ds(half * part, part)], o_ref.at[p], sems.at[p]
            )
            for p in range(count)
        ]
        for copy in copies:
            copy.start()
        for copy in copies:
            copy.wait()

    return pl.pallas_call(
        body,
        in_specs=[SMEM, ANY],
        out_specs=VMEM,
        out_shape=jax.ShapeDtypeStruct((count, part, width), BF16),
        scratch_shapes=[pltpu.SemaphoreType.DMA((count,))],
        compiler_params=params(),
        cost_estimate=cost(0, 2 << 20),
        name="spread",
    )(send_slot, neighbours)


def pick(blocks, index):
    rows, width = blocks.shape[1:]
    count = index.shape[0]

    def body(i_ref, b_ref, o_ref, sems):
        copies = [
            pltpu.make_async_copy(b_ref.at[i_ref[n]], o_ref.at[pl.ds(n * rows, rows)], sems.at[n])
            for n in range(count)
        ]
        for copy in copies:
            copy.start()
        for copy in copies:
            copy.wait()

    return pl.pallas_call(
        body,
        in_specs=[SMEM, ANY],
        out_specs=VMEM,
        out_shape=jax.ShapeDtypeStruct((count * rows, width), BF16),
        scratch_shapes=[pltpu.SemaphoreType.DMA((count,))],
        compiler_params=params(),
        cost_estimate=cost(0, 2 << 20),
        name="pick",
    )(index, blocks)


def sum_and_spread(terms, index):
    parts, total, width = terms[0].shape
    rows = NT // 2
    count = index.shape[0]

    def body(i_ref, *refs):
        t_refs, (o_ref, held, sems) = refs[: len(terms)], refs[len(terms) :]
        copies = []
        for h in range(parts):
            held[h] = sum(r[h].astype(F32) for r in t_refs).astype(BF16)
            for p in range(count):
                source = held.at[h, pl.ds(pl.multiple_of(i_ref[p] * rows, rows), rows)]
                copies.append(
                    pltpu.make_async_copy(source, o_ref.at[p, pl.ds(h * rows, rows)], sems.at[h, p])
                )
                copies[-1].start()
        wait_all(copies)

    return pl.pallas_call(
        body,
        in_specs=[SMEM] + [VMEM] * len(terms),
        out_specs=ANY,
        out_shape=jax.ShapeDtypeStruct((count, parts * rows, width), BF16),
        scratch_shapes=[pltpu.VMEM((parts, total, width), BF16), pltpu.SemaphoreType.DMA((parts, count))],
        compiler_params=params(),
        cost_estimate=cost(0, 5 << 20),
        name="sum_and_spread",
    )(index, *terms)


def settle(arrived, index, live):
    rows, width = arrived.shape[1:]
    count = index.shape[0]

    def body(i_ref, l_ref, a_ref, o_ref, sems):
        def copy(n):
            return pltpu.make_async_copy(a_ref.at[i_ref[n]], o_ref.at[pl.ds(n * rows, rows)], sems.at[n])

        for n in range(count):
            pl.when(l_ref[n] > 0)(lambda n=n: copy(n).start())
        for n in range(count):

            @pl.when(l_ref[n] == 0)
            def _():
                o_ref[n * rows : (n + 1) * rows, :] = jnp.zeros((rows, width), BF16)

            pl.when(l_ref[n] > 0)(lambda n=n: copy(n).wait())

    return pl.pallas_call(
        body,
        in_specs=[SMEM] * 2 + [ANY],
        out_specs=VMEM,
        out_shape=jax.ShapeDtypeStruct((count * rows, width), BF16),
        scratch_shapes=[pltpu.SemaphoreType.DMA((count,))],
        compiler_params=params(),
        cost_estimate=cost(0, 2 << 20),
        name="settle",
    )(index, live, arrived)


def add_into(bases, extras):
    count = len(bases)

    def body(*refs):
        for n in range(count):
            b_ref, e_ref, o_ref = refs[n], refs[count + n], refs[2 * count + n]
            o_ref[...] = (b_ref[...].astype(F32) + e_ref[...].astype(F32)).astype(BF16)

    specs = [pl.BlockSpec((b.shape[0], b.shape[1] // 2, b.shape[2]), lambda i: (0, i, 0)) for b in bases]
    return pl.pallas_call(
        body,
        grid=(2,),
        in_specs=specs * 2,
        out_specs=specs,
        out_shape=[jax.ShapeDtypeStruct(b.shape, BF16) for b in bases],
        input_output_aliases={n: n for n in range(count)},
        compiler_params=params(),
        cost_estimate=cost(0, 2 * count << 20),
        name="add_into",
    )(*bases, *extras)


def read_in(sources, places, sems):
    copies = [pltpu.make_async_copy(a, b, sems.at[n]) for n, (a, b) in enumerate(zip(sources, places))]
    for copy in copies:
        copy.start()
    return copies


def wait_all(copies):
    for copy in copies:
        copy.wait()


def project_into(begin, piece_refs, k_ref, v_ref, all_ref, held, keys, values, acc, store, sems, out_sem):
    parts = len(piece_refs)
    rows, depth = piece_refs[0].shape
    width = k_ref.shape[1]
    waits = []
    for i in range(parts):
        span = pl.ds(i * depth, depth)
        source = pl.ds(pl.multiple_of(piece_block(i) * depth, depth), depth)
        waits.append(
            read_in(
                [piece_refs[i], k_ref.at[source], v_ref.at[source]],
                [held.at[:, span], keys.at[span], values.at[span]],
                sems.at[i],
            )
        )
    begun = begin()
    cuts = [0, parts // 2, parts]
    for lo, hi in zip(cuts[:-1], cuts[1:]):
        for i in range(lo, hi):
            wait_all(waits[i])
        span = slice(lo * depth, hi * depth)
        for n, w_ref in enumerate((keys, values)):
            cols = slice(n * width, (n + 1) * width)
            term = dot(held[:, span], w_ref[span, :], 1, 0)
            if lo == 0:
                acc[:, cols] = term
            else:
                store(cols, (acc[:, cols] + term).astype(BF16))
    chunk = all_ref.shape[2]
    outs = []
    for n in range(all_ref.shape[0]):
        outs.append(pltpu.make_async_copy(held.at[:, pl.ds(n * chunk, chunk)], all_ref.at[n], out_sem.at[n]))
        outs[-1].start()
    return begun, outs


def project_scratch(rows, parts, depth, width):
    return [
        pltpu.VMEM((rows, parts * depth), BF16),
        pltpu.VMEM((parts * depth, width), BF16),
        pltpu.VMEM((parts * depth, width), BF16),
        pltpu.VMEM((rows, 2 * width), F32),
        pltpu.SemaphoreType.DMA((parts, 3)),
        pltpu.SemaphoreType.DMA((parts * depth // 256,)),
    ]


def project(pieces, key_weight, value_weight):
    parts = len(pieces)
    rows, depth = pieces[0].shape
    width = key_weight.shape[1]

    def body(*refs):
        k_ref, v_ref, o_ref, all_ref, held, keys, values, acc, sems, out_sem = refs[parts:]

        def store(cols, value):
            o_ref[:, cols] = value

        _, last = project_into(
            lambda: None, refs[:parts], k_ref, v_ref, all_ref, held, keys, values, acc, store, sems, out_sem
        )
        wait_all(last)

    return pl.pallas_call(
        body,
        in_specs=[ANY] * (parts + 2),
        out_specs=[VMEM, ANY],
        out_shape=[
            jax.ShapeDtypeStruct((rows, 2 * width), BF16),
            jax.ShapeDtypeStruct((parts * depth // 256, rows, 256), BF16),
        ],
        scratch_shapes=project_scratch(rows, parts, depth, width),
        compiler_params=params(),
        cost_estimate=cost(4 * parts * rows * depth * width, 16 << 20),
        name="project",
    )(*pieces, key_weight, value_weight)


def project_attend(pieces, key_weight, value_weight, queries, out_grad, first_rows, first_all, lengths):
    parts = len(pieces)
    rows, depth = pieces[0].shape
    tokens, width = queries.shape
    blocks = tokens // BLOCK
    heads = width // HEAD
    span = NEIGH * NT
    part = span // 2
    sub = NT // 2
    scale = HEAD ** (-0.5)
    chunk = 256

    def body(len_ref, *refs):
        piece_refs, refs = refs[:parts], refs[parts:]
        k_ref, v_ref, q_in, g_in, a_in, all_in = refs[:6]
        all_ref, dq_out, p_out, t_out, key_out, value_out = refs[6:12]
        held, keys, values, acc, sems, out_sem = refs[12:18]
        q_ref, g_ref, a_ref, b_ref, dq_ref, p_ref, t_ref, key_ref, value_ref = refs[18:27]
        chunk_ref, in_sems, out_sems, chunk_sems = refs[27:]

        def store(cols, value):
            b_ref[:, cols] = value

        def begin():
            picks = [c for kind in (0, 1) for c in chunk_places(kind, FAR)]
            columns = [pl.ds(pl.multiple_of(c * chunk, chunk), chunk) for c in picks]
            early = read_in([q_in, g_in, a_in], [q_ref, g_ref, a_ref], in_sems)
            later = read_in([all_in.at[c] for c in picks], [chunk_ref.at[n] for n in range(8)], chunk_sems)
            return early, later, columns

        (early, later, columns), last = project_into(
            begin, piece_refs, k_ref, v_ref, all_ref, held, keys, values, acc, store, sems, out_sem
        )
        wait_all(early)
        column = lax.broadcasted_iota(jnp.int32, (BLOCK, span), 1)
        row = (column // part) * sub + column % sub
        left = (column % part) < sub
        key_cols = [slice(h * HEAD, (h + 1) * HEAD) for h in range(heads)]
        value_cols = [slice(width + h * HEAD, width + (h + 1) * HEAD) for h in range(heads)]
        for block in range(blocks):
            mine = slice(block * BLOCK, (block + 1) * BLOCK)
            first = slice(block * part, (block + 1) * part)
            second = slice(rows + block * part, rows + (block + 1) * part)
            limit = jnp.where(left, len_ref[block * NEIGH], len_ref[block * NEIGH + 1])
            valid = row < limit
            both = lambda cols: jnp.concatenate([a_ref[first, cols], b_ref[first, cols]], axis=0)
            q = [q_ref[mine, c] for c in key_cols]
            g = [g_ref[mine, c] for c in key_cols]
            k = [both(c) for c in key_cols]
            v = [both(c) for c in value_cols]
            scores = [dot(q[h], k[h], 1, 1) for h in range(heads)]
            prob_grad = [dot(g[h], v[h], 1, 1) for h in range(heads)]
            attention = []
            for h in range(heads):
                masked = jnp.where(valid, scores[h] * scale, -jnp.inf)
                raised = jnp.exp(masked - jnp.max(masked, axis=1, keepdims=True))
                attention.append(raised / jnp.sum(raised, axis=1, keepdims=True))
            low = [a.astype(BF16) for a in attention]
            score_grad = []
            for h in range(heads):
                delta = jnp.sum(low[h].astype(F32) * prob_grad[h], axis=1, keepdims=True)
                score_grad.append((attention[h] * (prob_grad[h] - delta) * scale).astype(BF16))
            for h in range(heads):
                dq_ref[mine, key_cols[h]] = dot(score_grad[h], k[h], 1, 0).astype(BF16)
            for cols, lhs, rhs in ((key_cols, score_grad, q), (value_cols, low, g)):
                for h in range(heads):
                    grad = dot(lhs[h], rhs[h], 0, 0).astype(BF16)
                    p_ref[0, first, cols[h]] = grad[:part]
                    p_ref[1, first, cols[h]] = grad[part:]
                    grad_t = dot(rhs[h], lhs[h], 0, 0).astype(BF16)
                    t_ref[cols[h], first] = grad_t[:, :part]
                    t_ref[cols[h], second] = grad_t[:, part:]
        outs = read_in([p_ref, t_ref, dq_ref], [p_out, t_out, dq_out], out_sems.at[pl.ds(0, 3)])
        wait_all(later)
        for kind, (w_ref, w_out) in enumerate(((key_ref, key_out), (value_ref, value_out))):
            columns_t = slice(kind * width, (kind + 1) * width)
            for n in range(4):
                term = dot(t_ref[columns_t, :rows], chunk_ref[4 * kind + n], 1, 0)
                term = term + dot(t_ref[columns_t, rows:], held[:, columns[4 * kind + n]], 1, 0)
                w_ref[n] = term.astype(BF16)
            outs += read_in([w_ref], [w_out], out_sems.at[pl.ds(3 + kind, 1)])
        wait_all(outs)
        wait_all(last)

    shapes = [
        jax.ShapeDtypeStruct((parts * depth // 256, rows, 256), BF16),
        jax.ShapeDtypeStruct((tokens, width), BF16),
        jax.ShapeDtypeStruct((2, rows, 2 * width), BF16),
        jax.ShapeDtypeStruct((2 * width, 2 * rows), BF16),
    ] + [jax.ShapeDtypeStruct((4, width, chunk), BF16)] * 2
    return pl.pallas_call(
        body,
        in_specs=[SMEM] + [ANY] * (parts + 6),
        out_specs=[ANY] * 6,
        out_shape=shapes,
        scratch_shapes=project_scratch(rows, parts, depth, width)
        + [pltpu.VMEM((tokens, width), BF16)] * 2
        + [pltpu.VMEM((rows, 2 * width), BF16)] * 2
        + [pltpu.VMEM(v.shape, BF16) for v in shapes[1:]]
        + [pltpu.VMEM((8, rows, chunk), BF16)]
        + [pltpu.SemaphoreType.DMA((n,)) for n in (3, 5, 8)],
        compiler_params=params(),
        cost_estimate=cost(4 * parts * rows * depth * width, 16 << 20),
        name="project_attend",
    )(lengths, *pieces, key_weight, value_weight, queries, out_grad, first_rows, first_all)


def weight_groups(grads_t, rows, jobs, name):
    chunk = 256
    both, count = grads_t.shape
    width, part, parts = both // 2, rows[0].shape[1], len(rows)
    chunks = 4 * len(jobs)
    shapes = [jax.ShapeDtypeStruct((4, width, chunk), BF16)] * len(jobs)

    def body(t_in, *refs):
        r_refs, o_refs = refs[:parts], refs[parts : parts + len(jobs)]
        t_ref, held, out_held, t_sem, r_sems, o_sems = refs[parts + len(jobs) :]
        t_copy = pltpu.make_async_copy(t_in, t_ref, t_sem)
        t_copy.start()
        copies = []
        for n, place in enumerate([c for job in jobs for c in chunk_places(*job)]):
            copies.append(
                read_in(
                    [r.at[place] for r in r_refs],
                    [held.at[n, pl.ds(h * part, part)] for h in range(parts)],
                    r_sems.at[n],
                )
            )
        t_copy.wait()
        outs, at = [], 0
        for job, (half, _) in enumerate(jobs):
            total = 4
            for j in range(total):
                wait_all(copies[at + j])
            for j in range(total):
                lhs = t_ref[half * width : (half + 1) * width, :]
                out_held[at + j] = dot(lhs, held[at + j], 1, 0).astype(BF16)
            outs += read_in([out_held.at[pl.ds(at, total)]], [o_refs[job]], o_sems.at[pl.ds(job, 1)])
            at += total
        wait_all(outs)

    return pl.pallas_call(
        body,
        in_specs=[ANY] * (1 + parts),
        out_specs=[ANY] * len(jobs),
        out_shape=shapes,
        scratch_shapes=[
            pltpu.VMEM((both, count), BF16),
            pltpu.VMEM((chunks, count, chunk), BF16),
            pltpu.VMEM((chunks, width, chunk), BF16),
            pltpu.SemaphoreType.DMA,
            pltpu.SemaphoreType.DMA((chunks, parts)),
            pltpu.SemaphoreType.DMA((len(jobs),)),
        ],
        compiler_params=params(),
        cost_estimate=cost(2 * chunks * width * count * chunk, chunks * 3 << 18),
        name=name,
    )(grads_t, *rows)


def row_blocks(pairs, weights, steps, name):
    tile = 512
    halves, rows, both = pairs[0].shape
    width = both // 2
    count = len(steps)

    def body(*refs):
        p_in, w_in, o_refs = refs[:2], refs[2:6], refs[6 : 6 + count]
        p_ref, w_ref, o_held, p_sems, w_sems, o_sems = refs[6 + count :]
        p_copies = read_in(p_in, [p_ref.at[:, :, pl.ds(n * both, both)] for n in range(2)], p_sems)
        w_copies = []
        for n, step in enumerate(steps):
            chip = moved(here()[2], step)
            span = pl.ds(pl.multiple_of((2 * chip + here()[3]) * tile, tile), tile)
            sources = [w.at[span] for w in w_in]
            w_copies.append(
                read_in(sources, [w_ref.at[n, :, pl.ds(m * width, width)] for m in range(4)], w_sems.at[n])
            )
        wait_all(p_copies)
        outs = []
        for n in range(count):
            wait_all(w_copies[n])
            for h in range(halves):
                o_held[n, h] = dot(p_ref[h], w_ref[n], 1, 1).astype(BF16)
            outs += read_in([o_held.at[n]], [o_refs[n]], o_sems.at[pl.ds(n, 1)])
        wait_all(outs)

    return pl.pallas_call(
        body,
        in_specs=[ANY] * 6,
        out_specs=[ANY] * count,
        out_shape=[jax.ShapeDtypeStruct((halves, rows, tile), BF16)] * count,
        scratch_shapes=[
            pltpu.VMEM((halves, rows, 2 * both), BF16),
            pltpu.VMEM((count, tile, 2 * both), BF16),
            pltpu.VMEM((count, halves, rows, tile), BF16),
            pltpu.SemaphoreType.DMA((2,)),
            pltpu.SemaphoreType.DMA((count, 4)),
            pltpu.SemaphoreType.DMA((count,)),
        ],
        compiler_params=params(),
        cost_estimate=cost(4 * count * halves * rows * tile * both, (2 + 2 * count) << 20),
        name=name,
    )(*pairs, *weights)


def turn(value, axis, sign):
    def to(i):
        z, x, y, core = i // 32, i // 8 % 4, i // 2 % 4, i % 2
        step = sign * (1 - 2 * core)
        if axis == "z":
            z = (z + step) % 4
        elif axis == "x":
            x = (x + step) % 4
        else:
            y = (y + step) % 4
        return ((z * 4 + x) * 4 + y) * 2 + core

    return lax.ppermute(value, ("seq", "tensor"), [(i, to(i)) for i in range(128)])


def swap(value):
    return lax.ppermute(value, "tensor", [(i, i ^ 1) for i in range(8)])


def after(value, *deps):
    return lax.optimization_barrier((value,) + deps)[0]


def ring_sums(own, first, second, name):
    _, width, chunk = own[0].shape

    def body(*refs):
        for n in range(2):
            ins, outs = refs[3 * n : 3 * n + 3], refs[6 + 4 * n : 10 + 4 * n]
            for j in range(4):
                value = sum(r[j].astype(F32) for r in ins)
                outs[j][...] = value if j == 3 else value.astype(BF16)

    whole = VMEM
    shapes = [jax.ShapeDtypeStruct((1, width, chunk), BF16)] * 3 + [jax.ShapeDtypeStruct((1, width, chunk), F32)]
    return pl.pallas_call(
        lambda *refs: body(*refs[:6], *[r.at[0] for r in refs[6:]]),
        in_specs=[whole] * 6,
        out_specs=[whole] * 8,
        out_shape=shapes * 2,
        compiler_params=params(),
        cost_estimate=cost(0, 10 << 20),
        name=name,
    )(own[0], first[0], second[0], own[1], first[1], second[1])


def gather_rows(own, last):
    near = turn(own, "y", 1)
    away = turn(own, "y", -1)
    far = turn(near, "y", 1)
    other = after(far, *last) if last else far
    return [own, swap(own), near, swap(near), away, swap(away), far, swap(other)], near


def local(queries, out_grad, neighbours, key_weight, value_weight, owner, slot, lengths):
    seq_count = lax.axis_size("seq")
    position = lax.axis_index("seq")
    core = here()[3]
    slot_count = lengths.shape[1]
    width = key_weight.shape[1]
    holders = owner.reshape(seq_count, -1)
    slots = slot.reshape(seq_count, -1)
    refs = holders.shape[1]
    order = jnp.arange(refs, dtype=jnp.int32)
    readers = jnp.arange(seq_count, dtype=jnp.int32)

    mine = holders == position
    send_slot = jnp.sum(jnp.where(mine, slots, 0), axis=1)
    my_holder = lax.dynamic_index_in_dim(holders, position, 0, keepdims=False)
    my_slot = lax.dynamic_index_in_dim(slots, position, 0, keepdims=False)
    my_lengths = jnp.take(lengths.reshape(-1), my_holder * slot_count + my_slot, mode="clip")
    back_ref = jnp.sum(jnp.where(my_holder[:, None] == readers[None, :], order[:, None], 0), axis=0)
    reads = mine[:, :, None] & (slots[:, :, None] == jnp.arange(slot_count, dtype=jnp.int32))
    slot_reader = jnp.sum(jnp.where(reads, readers[:, None, None], 0), axis=(0, 1))
    slot_live = jnp.any(reads, axis=(0, 1)).astype(jnp.int32)

    by_slot = neighbours.reshape(slot_count, NT, width)
    got_a = lax.all_to_all(spread(by_slot, send_slot, 0), "seq", split_axis=0, concat_axis=0, tiled=True)
    other_weights = [swap(key_weight), swap(value_weight)]
    send_b = after(spread(by_slot, send_slot, 1), got_a)
    got_b = lax.all_to_all(send_b, "seq", split_axis=0, concat_axis=0, tiled=True)
    rows_a, near_a = gather_rows(pick(got_a, my_holder), ())
    pair_a, all_a = project(rows_a, key_weight, value_weight)
    rows_b, _ = gather_rows(pick(after(got_b, near_a, *other_weights), my_holder), (pair_a,))
    all_b, query_grad, pair, pair_t, kf, vf = project_attend(
        rows_b, key_weight, value_weight, queries, out_grad, pair_a, all_a, my_lengths
    )

    def rows_of(earlier, steps, name):
        pairs = [after(pair, *earlier), other_pair] if earlier else [pair, other_pair]
        return row_blocks(pairs, [key_weight, value_weight] + other_weights, steps, name)

    other_pair = swap(pair)
    far_x, far_z = turn(kf, "x", 1), turn(vf, "z", 1)
    kn, vn, km, vm, ko, vo = weight_groups(
        pair_t, [all_a, all_b], [(kind, step) for step in (BACK, ON, OWN) for kind in (0, 1)], "weight_rest"
    )
    back = [turn(after(kn, far_x), "x", -1), turn(after(vn, far_z), "z", -1)]
    km, vm = add_into([km, vm], [far_x, far_z])
    (t2,) = rows_of((km,), [FAR], "row_far")
    far_y = turn(t2, "y", 1)
    tn, tm, t0 = rows_of((t2,), [BACK, ON, OWN], "row_next")
    back_y = turn(tn, "y", -1)
    (tm,) = add_into([tm], [after(far_y, tn)])
    onward_y = turn(tm, "y", 1)
    onward = [turn(after(km, back[0], tn), "x", 1), turn(after(vm, back[1], tn), "z", 1)]

    returning = sum_and_spread([t0, back_y, onward_y], back_ref)
    arrived = lax.all_to_all(returning, "seq", split_axis=0, concat_axis=0, tiled=True)
    neighbour_grad = settle(arrived, slot_reader, slot_live)

    kf, kn, km, k0, vf, vn, vm, v0 = ring_sums([ko, vo], back, onward, "ring_sums")
    came = [turn(kf, "z", 1), turn(vf, "x", 1)]
    back = [turn(kn, "z", -1), turn(vn, "x", -1)]
    km, vm = add_into([km, vm], came)
    onward = [turn(km, "z", 1), turn(vm, "x", 1)]
    done = [
        (mine + one.astype(F32) + other.astype(F32))[0].T
        for mine, one, other in zip((k0, v0), back, onward)
    ]
    return (query_grad, done[0], done[1], neighbour_grad)


def solution(mesh):
    placed = (
        P("seq", "tensor"),
        P("seq", "tensor"),
        P("seq", "tensor"),
        P(None, "tensor"),
        P(None, "tensor"),
        P(),
        P(),
        P(),
    )
    return jax.shard_map(
        local,
        mesh=mesh,
        in_specs=placed,
        out_specs=(P("seq", "tensor"), P("seq", "tensor"), P("seq", "tensor"), P("seq", "tensor")),
        check_vma=False,
    )
```

```python
import jax
import jax.numpy as jnp
from jax import lax
from jax.experimental import pallas as pl
from jax.experimental.pallas import tpu as pltpu
from jax.sharding import PartitionSpec as P

HEAD = 128
BLOCK = 64
NT = 128
NEIGH = 2
VMEM_LIMIT = 60 * 1024 * 1024
SMALL_LIMIT = 12 * 1024 * 1024
F32 = jnp.float32
BF16 = jnp.bfloat16


def params(limit=VMEM_LIMIT):
    return pltpu.CompilerParams(vmem_limit_bytes=limit)


def cost(flops, moved):
    return pl.CostEstimate(flops=flops // 1024, bytes_accessed=moved // 1024, transcendentals=0)


def dot(a, b, ca, cb):
    return lax.dot_general(a, b, (((ca,), (cb,)), ((), ())), preferred_element_type=F32)


ANY = pl.BlockSpec(memory_space=pl.ANY)
VMEM = pl.BlockSpec(memory_space=pltpu.VMEM)
SMEM = pl.BlockSpec(memory_space=pltpu.SMEM)


FAR, BACK, ON, OWN = 0, 1, 2, 3


def here():
    spot, column = lax.axis_index("seq"), lax.axis_index("tensor")
    return spot >> 2, spot & 3, column >> 1, column & 1


def moved(at, step):
    way = 1 - 2 * here()[3]
    return (at + (2, -way, way, 0)[step]) & 3


def piece_block(n):
    core = here()[3]
    step, other = ((OWN, 0), (OWN, 1), (BACK, 0), (ON, 1), (ON, 0), (BACK, 1), (FAR, 0), (FAR, 1))[n]
    return 2 * moved(here()[2], step) + (core ^ other)


def chunk_place(z, x):
    _, _, y, core = here()
    step, other = (z - y) & 3, (x >> 1) ^ core
    behind = step == moved(0, BACK)
    piece = jnp.where(
        step == 0,
        other,
        jnp.where(step == 2, 6 + other, jnp.where(behind, jnp.where(other == 1, 5, 2), jnp.where(other == 1, 3, 4))),
    )
    return 2 * piece + (x & 1)


def chunk_places(kind, step):
    z, x, _, _ = here()
    if kind == 0:
        return [chunk_place(moved(z, n), moved(x, step)) for n in range(4)]
    return [chunk_place(moved(z, step), moved(x, n)) for n in range(4)]


def spread(neighbours, send_slot, half):
    slots, rows, width = neighbours.shape
    count, part = send_slot.shape[0], rows // 2

    def body(s_ref, n_ref, o_ref, sems):
        copies = [
            pltpu.make_async_copy(
                n_ref.at[s_ref[p], pl.ds(half * part, part)], o_ref.at[p], sems.at[p]
            )
            for p in range(count)
        ]
        for copy in copies:
            copy.start()
        for copy in copies:
            copy.wait()

    return pl.pallas_call(
        body,
        in_specs=[SMEM, ANY],
        out_specs=VMEM,
        out_shape=jax.ShapeDtypeStruct((count, part, width), BF16),
        scratch_shapes=[pltpu.SemaphoreType.DMA((count,))],
        compiler_params=params(),
        cost_estimate=cost(0, 2 << 20),
        name="spread",
    )(send_slot, neighbours)


def pick(blocks, index):
    rows, width = blocks.shape[1:]
    count = index.shape[0]

    def body(i_ref, b_ref, o_ref, sems):
        copies = [
            pltpu.make_async_copy(b_ref.at[i_ref[n]], o_ref.at[pl.ds(n * rows, rows)], sems.at[n])
            for n in range(count)
        ]
        for copy in copies:
            copy.start()
        for copy in copies:
            copy.wait()

    return pl.pallas_call(
        body,
        in_specs=[SMEM, ANY],
        out_specs=VMEM,
        out_shape=jax.ShapeDtypeStruct((count * rows, width), BF16),
        scratch_shapes=[pltpu.SemaphoreType.DMA((count,))],
        compiler_params=params(SMALL_LIMIT),
        cost_estimate=cost(0, 2 << 20),
        name="pick",
    )(index, blocks)


def sum_and_spread(terms, index):
    parts, total, width = terms[0].shape
    rows = NT // 2
    count = index.shape[0]

    def body(i_ref, *refs):
        t_refs, (o_ref, held, sems) = refs[: len(terms)], refs[len(terms) :]
        copies = []
        for h in range(parts):
            held[h] = sum(r[h].astype(F32) for r in t_refs).astype(BF16)
            for p in range(count):
                source = held.at[h, pl.ds(pl.multiple_of(i_ref[p] * rows, rows), rows)]
                copies.append(
                    pltpu.make_async_copy(source, o_ref.at[p, pl.ds(h * rows, rows)], sems.at[h, p])
                )
                copies[-1].start()
        wait_all(copies)

    return pl.pallas_call(
        body,
        in_specs=[SMEM] + [VMEM] * len(terms),
        out_specs=ANY,
        out_shape=jax.ShapeDtypeStruct((count, parts * rows, width), BF16),
        scratch_shapes=[pltpu.VMEM((parts, total, width), BF16), pltpu.SemaphoreType.DMA((parts, count))],
        compiler_params=params(),
        cost_estimate=cost(0, 5 << 20),
        name="sum_and_spread",
    )(index, *terms)


def settle(arrived, index, live):
    rows, width = arrived.shape[1:]
    count = index.shape[0]

    def body(i_ref, l_ref, a_ref, o_ref, sems):
        def copy(n):
            return pltpu.make_async_copy(a_ref.at[i_ref[n]], o_ref.at[pl.ds(n * rows, rows)], sems.at[n])

        for n in range(count):
            pl.when(l_ref[n] > 0)(lambda n=n: copy(n).start())
        for n in range(count):

            @pl.when(l_ref[n] == 0)
            def _():
                o_ref[n * rows : (n + 1) * rows, :] = jnp.zeros((rows, width), BF16)

            pl.when(l_ref[n] > 0)(lambda n=n: copy(n).wait())

    return pl.pallas_call(
        body,
        in_specs=[SMEM] * 2 + [ANY],
        out_specs=VMEM,
        out_shape=jax.ShapeDtypeStruct((count * rows, width), BF16),
        scratch_shapes=[pltpu.SemaphoreType.DMA((count,))],
        compiler_params=params(SMALL_LIMIT),
        cost_estimate=cost(0, 2 << 20),
        name="settle",
    )(index, live, arrived)


def add_into(bases, extras):
    count = len(bases)

    def body(*refs):
        for n in range(count):
            b_ref, e_ref, o_ref = refs[n], refs[count + n], refs[2 * count + n]
            o_ref[...] = (b_ref[...].astype(F32) + e_ref[...].astype(F32)).astype(BF16)

    specs = [pl.BlockSpec((b.shape[0], b.shape[1] // 2, b.shape[2]), lambda i: (0, i, 0)) for b in bases]
    return pl.pallas_call(
        body,
        grid=(2,),
        in_specs=specs * 2,
        out_specs=specs,
        out_shape=[jax.ShapeDtypeStruct(b.shape, BF16) for b in bases],
        input_output_aliases={n: n for n in range(count)},
        compiler_params=params(),
        cost_estimate=cost(0, 2 * count << 20),
        name="add_into",
    )(*bases, *extras)


def read_in(sources, places, sems):
    copies = [pltpu.make_async_copy(a, b, sems.at[n]) for n, (a, b) in enumerate(zip(sources, places))]
    for copy in copies:
        copy.start()
    return copies


def wait_all(copies):
    for copy in copies:
        copy.wait()


def project_into(begin, piece_refs, k_ref, v_ref, all_ref, held, keys, values, acc, store, sems, out_sem):
    parts = len(piece_refs)
    rows, depth = piece_refs[0].shape
    width = k_ref.shape[1]
    waits = []
    for i in range(parts):
        span = pl.ds(i * depth, depth)
        source = pl.ds(pl.multiple_of(piece_block(i) * depth, depth), depth)
        waits.append(
            read_in(
                [piece_refs[i], k_ref.at[source], v_ref.at[source]],
                [held.at[:, span], keys.at[span], values.at[span]],
                sems.at[i],
            )
        )
    begun = begin()
    cuts = [0, parts // 2, parts]
    for lo, hi in zip(cuts[:-1], cuts[1:]):
        for i in range(lo, hi):
            wait_all(waits[i])
        span = slice(lo * depth, hi * depth)
        for n, w_ref in enumerate((keys, values)):
            cols = slice(n * width, (n + 1) * width)
            term = dot(held[:, span], w_ref[span, :], 1, 0)
            if lo == 0:
                acc[:, cols] = term
            else:
                store(cols, (acc[:, cols] + term).astype(BF16))
    chunk = all_ref.shape[2]
    outs = []
    for n in range(all_ref.shape[0]):
        outs.append(pltpu.make_async_copy(held.at[:, pl.ds(n * chunk, chunk)], all_ref.at[n], out_sem.at[n]))
        outs[-1].start()
    return begun, outs


def project_scratch(rows, parts, depth, width):
    return [
        pltpu.VMEM((rows, parts * depth), BF16),
        pltpu.VMEM((parts * depth, width), BF16),
        pltpu.VMEM((parts * depth, width), BF16),
        pltpu.VMEM((rows, 2 * width), F32),
        pltpu.SemaphoreType.DMA((parts, 3)),
        pltpu.SemaphoreType.DMA((parts * depth // 256,)),
    ]


def project(pieces, key_weight, value_weight):
    parts = len(pieces)
    rows, depth = pieces[0].shape
    width = key_weight.shape[1]

    def body(*refs):
        k_ref, v_ref, o_ref, all_ref, held, keys, values, acc, sems, out_sem = refs[parts:]

        def store(cols, value):
            o_ref[:, cols] = value

        _, last = project_into(
            lambda: None, refs[:parts], k_ref, v_ref, all_ref, held, keys, values, acc, store, sems, out_sem
        )
        wait_all(last)

    return pl.pallas_call(
        body,
        in_specs=[ANY] * (parts + 2),
        out_specs=[VMEM, ANY],
        out_shape=[
            jax.ShapeDtypeStruct((rows, 2 * width), BF16),
            jax.ShapeDtypeStruct((parts * depth // 256, rows, 256), BF16),
        ],
        scratch_shapes=project_scratch(rows, parts, depth, width),
        compiler_params=params(),
        cost_estimate=cost(4 * parts * rows * depth * width, 16 << 20),
        name="project",
    )(*pieces, key_weight, value_weight)


def project_attend(pieces, key_weight, value_weight, queries, out_grad, first_rows, lengths):
    parts = len(pieces)
    rows, depth = pieces[0].shape
    tokens, width = queries.shape
    blocks = tokens // BLOCK
    heads = width // HEAD
    span = NEIGH * NT
    part = span // 2
    sub = NT // 2
    scale = HEAD ** (-0.5)

    def body(len_ref, *refs):
        piece_refs, refs = refs[:parts], refs[parts:]
        k_ref, v_ref, q_in, g_in, a_in = refs[:5]
        all_ref, dq_out, p_out, t_out = refs[5:9]
        held, keys, values, acc, sems, out_sem = refs[9:15]
        q_ref, g_ref, a_ref, b_ref, dq_ref, p_ref, t_ref, in_sems, out_sems = refs[15:]

        def store(cols, value):
            b_ref[:, cols] = value

        def begin():
            return read_in([q_in, g_in, a_in], [q_ref, g_ref, a_ref], in_sems)

        early, last = project_into(
            begin, piece_refs, k_ref, v_ref, all_ref, held, keys, values, acc, store, sems, out_sem
        )
        wait_all(early)
        column = lax.broadcasted_iota(jnp.int32, (BLOCK, span), 1)
        row = (column // part) * sub + column % sub
        left = (column % part) < sub
        key_cols = [slice(h * HEAD, (h + 1) * HEAD) for h in range(heads)]
        value_cols = [slice(width + h * HEAD, width + (h + 1) * HEAD) for h in range(heads)]
        for block in range(blocks):
            mine = slice(block * BLOCK, (block + 1) * BLOCK)
            first = slice(block * part, (block + 1) * part)
            second = slice(rows + block * part, rows + (block + 1) * part)
            limit = jnp.where(left, len_ref[block * NEIGH], len_ref[block * NEIGH + 1])
            valid = row < limit
            both = lambda cols: jnp.concatenate([a_ref[first, cols], b_ref[first, cols]], axis=0)
            q = [q_ref[mine, c] for c in key_cols]
            g = [g_ref[mine, c] for c in key_cols]
            k = [both(c) for c in key_cols]
            v = [both(c) for c in value_cols]
            scores = [dot(q[h], k[h], 1, 1) for h in range(heads)]
            prob_grad = [dot(g[h], v[h], 1, 1) for h in range(heads)]
            attention = []
            for h in range(heads):
                masked = jnp.where(valid, scores[h] * scale, -jnp.inf)
                raised = jnp.exp(masked - jnp.max(masked, axis=1, keepdims=True))
                attention.append(raised / jnp.sum(raised, axis=1, keepdims=True))
            low = [a.astype(BF16) for a in attention]
            score_grad = []
            for h in range(heads):
                delta = jnp.sum(low[h].astype(F32) * prob_grad[h], axis=1, keepdims=True)
                score_grad.append((attention[h] * (prob_grad[h] - delta) * scale).astype(BF16))
            for h in range(heads):
                dq_ref[mine, key_cols[h]] = dot(score_grad[h], k[h], 1, 0).astype(BF16)
            for cols, lhs, rhs in ((key_cols, score_grad, q), (value_cols, low, g)):
                for h in range(heads):
                    grad = dot(lhs[h], rhs[h], 0, 0).astype(BF16)
                    p_ref[0, first, cols[h]] = grad[:part]
                    p_ref[1, first, cols[h]] = grad[part:]
                    grad_t = dot(rhs[h], lhs[h], 0, 0).astype(BF16)
                    t_ref[cols[h], first] = grad_t[:, :part]
                    t_ref[cols[h], second] = grad_t[:, part:]
        outs = read_in([p_ref, t_ref, dq_ref], [p_out, t_out, dq_out], out_sems)
        wait_all(outs)
        wait_all(last)

    shapes = [
        jax.ShapeDtypeStruct((parts * depth // 256, rows, 256), BF16),
        jax.ShapeDtypeStruct((tokens, width), BF16),
        jax.ShapeDtypeStruct((2, rows, 2 * width), BF16),
        jax.ShapeDtypeStruct((2 * width, 2 * rows), BF16),
    ]
    return pl.pallas_call(
        body,
        in_specs=[SMEM] + [ANY] * (parts + 5),
        out_specs=[ANY] * 4,
        out_shape=shapes,
        scratch_shapes=project_scratch(rows, parts, depth, width)
        + [pltpu.VMEM((tokens, width), BF16)] * 2
        + [pltpu.VMEM((rows, 2 * width), BF16)] * 2
        + [pltpu.VMEM(v.shape, BF16) for v in shapes[1:]]
        + [pltpu.SemaphoreType.DMA((3,))] * 2,
        compiler_params=params(),
        cost_estimate=cost(4 * parts * rows * depth * width, 16 << 20),
        name="project_attend",
    )(lengths, *pieces, key_weight, value_weight, queries, out_grad, first_rows)


def weight_groups(grads_t, rows, jobs, name):
    chunk = 256
    both, count = grads_t.shape
    width, part, parts = both // 2, rows[0].shape[1], len(rows)
    chunks = 4 * len(jobs)
    shapes = [jax.ShapeDtypeStruct((4, width, chunk), BF16)] * len(jobs)

    def body(t_in, *refs):
        r_refs, o_refs = refs[:parts], refs[parts : parts + len(jobs)]
        t_ref, held, out_held, t_sem, r_sems, o_sems = refs[parts + len(jobs) :]
        t_copy = pltpu.make_async_copy(t_in, t_ref, t_sem)
        t_copy.start()
        copies = []
        for n, place in enumerate([c for job in jobs for c in chunk_places(*job)]):
            copies.append(
                read_in(
                    [r.at[place] for r in r_refs],
                    [held.at[n, pl.ds(h * part, part)] for h in range(parts)],
                    r_sems.at[n],
                )
            )
        t_copy.wait()
        outs, at = [], 0
        for job, (half, _) in enumerate(jobs):
            total = 4
            for j in range(total):
                wait_all(copies[at + j])
            for j in range(total):
                lhs = t_ref[half * width : (half + 1) * width, :]
                out_held[at + j] = dot(lhs, held[at + j], 1, 0).astype(BF16)
            outs += read_in([out_held.at[pl.ds(at, total)]], [o_refs[job]], o_sems.at[pl.ds(job, 1)])
            at += total
        wait_all(outs)

    return pl.pallas_call(
        body,
        in_specs=[ANY] * (1 + parts),
        out_specs=[ANY] * len(jobs),
        out_shape=shapes,
        scratch_shapes=[
            pltpu.VMEM((both, count), BF16),
            pltpu.VMEM((chunks, count, chunk), BF16),
            pltpu.VMEM((chunks, width, chunk), BF16),
            pltpu.SemaphoreType.DMA,
            pltpu.SemaphoreType.DMA((chunks, parts)),
            pltpu.SemaphoreType.DMA((len(jobs),)),
        ],
        compiler_params=params(),
        cost_estimate=cost(2 * chunks * width * count * chunk, chunks * 3 << 18),
        name=name,
    )(grads_t, *rows)


def row_blocks(pairs, weights, steps, name):
    tile = 512
    halves, rows, both = pairs[0].shape
    width = both // 2
    count = len(steps)

    def body(*refs):
        p_in, w_in, o_refs = refs[:2], refs[2:6], refs[6 : 6 + count]
        p_ref, w_ref, o_held, p_sems, w_sems, o_sems = refs[6 + count :]
        p_copies = read_in(p_in, [p_ref.at[:, :, pl.ds(n * both, both)] for n in range(2)], p_sems)
        w_copies = []
        for n, step in enumerate(steps):
            chip = moved(here()[2], step)
            span = pl.ds(pl.multiple_of((2 * chip + here()[3]) * tile, tile), tile)
            sources = [w.at[span] for w in w_in]
            w_copies.append(
                read_in(sources, [w_ref.at[n, :, pl.ds(m * width, width)] for m in range(4)], w_sems.at[n])
            )
        wait_all(p_copies)
        outs = []
        for n in range(count):
            wait_all(w_copies[n])
            for h in range(halves):
                o_held[n, h] = dot(p_ref[h], w_ref[n], 1, 1).astype(BF16)
            outs += read_in([o_held.at[n]], [o_refs[n]], o_sems.at[pl.ds(n, 1)])
        wait_all(outs)

    return pl.pallas_call(
        body,
        in_specs=[ANY] * 6,
        out_specs=[ANY] * count,
        out_shape=[jax.ShapeDtypeStruct((halves, rows, tile), BF16)] * count,
        scratch_shapes=[
            pltpu.VMEM((halves, rows, 2 * both), BF16),
            pltpu.VMEM((count, tile, 2 * both), BF16),
            pltpu.VMEM((count, halves, rows, tile), BF16),
            pltpu.SemaphoreType.DMA((2,)),
            pltpu.SemaphoreType.DMA((count, 4)),
            pltpu.SemaphoreType.DMA((count,)),
        ],
        compiler_params=params(),
        cost_estimate=cost(4 * count * halves * rows * tile * both, (2 + 2 * count) << 20),
        name=name,
    )(*pairs, *weights)


def turn(value, axis, sign):
    def to(i):
        z, x, y, core = i // 32, i // 8 % 4, i // 2 % 4, i % 2
        step = sign * (1 - 2 * core)
        if axis == "z":
            z = (z + step) % 4
        elif axis == "x":
            x = (x + step) % 4
        else:
            y = (y + step) % 4
        return ((z * 4 + x) * 4 + y) * 2 + core

    return lax.ppermute(value, ("seq", "tensor"), [(i, to(i)) for i in range(128)])


def jump(value, axis):
    to = lambda i: i ^ 8 if axis == "z" else i ^ 2
    return lax.ppermute(value, "seq", [(i, to(i)) for i in range(16)])


def swap(value):
    return lax.ppermute(value, "tensor", [(i, i ^ 1) for i in range(8)])


def after(value, *deps):
    return lax.optimization_barrier((value,) + deps)[0]


def ring_sums(own, first, second, name):
    _, width, chunk = own[0].shape

    def body(*refs):
        for n in range(2):
            ins, outs = refs[3 * n : 3 * n + 3], refs[6 + 4 * n : 10 + 4 * n]
            for j in range(4):
                value = sum(r[j].astype(F32) for r in ins)
                outs[j][...] = value if j == 3 else value.astype(BF16)

    whole = VMEM
    shapes = [jax.ShapeDtypeStruct((1, width, chunk), BF16)] * 3 + [jax.ShapeDtypeStruct((1, width, chunk), F32)]
    return pl.pallas_call(
        lambda *refs: body(*refs[:6], *[r.at[0] for r in refs[6:]]),
        in_specs=[whole] * 6,
        out_specs=[whole] * 8,
        out_shape=shapes * 2,
        compiler_params=params(),
        cost_estimate=cost(0, 10 << 20),
        name=name,
    )(own[0], first[0], second[0], own[1], first[1], second[1])


def gather_rows(own, last):
    near = turn(own, "y", 1)
    away = turn(own, "y", -1)
    far = turn(near, "y", 1)
    other = after(far, *last) if last else far
    return [own, swap(own), near, swap(near), away, swap(away), far, swap(other)], near


def local(queries, out_grad, neighbours, key_weight, value_weight, owner, slot, lengths):
    seq_count = lax.axis_size("seq")
    position = lax.axis_index("seq")
    core = here()[3]
    slot_count = lengths.shape[1]
    width = key_weight.shape[1]
    holders = owner.reshape(seq_count, -1)
    slots = slot.reshape(seq_count, -1)
    refs = holders.shape[1]
    order = jnp.arange(refs, dtype=jnp.int32)
    readers = jnp.arange(seq_count, dtype=jnp.int32)

    mine = holders == position
    send_slot = jnp.sum(jnp.where(mine, slots, 0), axis=1)
    my_holder = lax.dynamic_index_in_dim(holders, position, 0, keepdims=False)
    my_slot = lax.dynamic_index_in_dim(slots, position, 0, keepdims=False)
    my_lengths = jnp.take(lengths.reshape(-1), my_holder * slot_count + my_slot, mode="clip")
    back_ref = jnp.sum(jnp.where(my_holder[:, None] == readers[None, :], order[:, None], 0), axis=0)
    reads = mine[:, :, None] & (slots[:, :, None] == jnp.arange(slot_count, dtype=jnp.int32))
    slot_reader = jnp.sum(jnp.where(reads, readers[:, None, None], 0), axis=(0, 1))
    slot_live = jnp.any(reads, axis=(0, 1)).astype(jnp.int32)

    by_slot = neighbours.reshape(slot_count, NT, width)
    got_a = lax.all_to_all(spread(by_slot, send_slot, 0), "seq", split_axis=0, concat_axis=0, tiled=True)
    other_weights = [swap(key_weight), swap(value_weight)]
    send_b = after(spread(by_slot, send_slot, 1), got_a)
    got_b = lax.all_to_all(send_b, "seq", split_axis=0, concat_axis=0, tiled=True)
    rows_a, near_a = gather_rows(pick(got_a, my_holder), ())
    pair_a, all_a = project(rows_a, key_weight, value_weight)
    rows_b, _ = gather_rows(pick(after(got_b, near_a, my_lengths, *other_weights), my_holder), (pair_a,))
    all_b, query_grad, pair, pair_t = project_attend(
        rows_b, key_weight, value_weight, queries, out_grad, pair_a, my_lengths
    )

    def rows_of(earlier, steps, name):
        pairs = [after(pair, *earlier), other_pair] if earlier else [pair, other_pair]
        return row_blocks(pairs, [key_weight, value_weight] + other_weights, steps, name)

    other_pair = swap(pair)
    rows = [all_a, all_b]
    kf, vf, kn, vn = weight_groups(
        pair_t, rows, [(kind, step) for step in (FAR, BACK) for kind in (0, 1)], "weight_far"
    )
    far_x, far_z = turn(kf, "x", 1), turn(vf, "z", 1)
    (t2,) = rows_of((kf,), [FAR], "row_far")
    far_y = turn(t2, "y", 1)
    tn, tm, t0 = rows_of((t2,), [BACK, ON, OWN], "row_next")
    back_y = turn(tn, "y", -1)
    (tm,) = add_into([after(tm, tn, far_x, far_z)], [far_y])
    onward_y = turn(tm, "y", 1)
    back = [turn(after(kn, far_x, tm), "x", -1), turn(after(vn, far_z, tm), "z", -1)]
    km, vm, ko, vo = weight_groups(
        after(pair_t, tm), rows, [(kind, step) for step in (ON, OWN) for kind in (0, 1)], "weight_rest"
    )
    km, vm = add_into([after(km, tm, *back), vm], [far_x, far_z])
    onward = [turn(km, "x", 1), turn(vm, "z", 1)]

    kf, kn, km, k0, vf, vn, vm, v0 = ring_sums([ko, vo], back, onward, "ring_sums")
    came = [
        [jump(far, axis), turn(behind, axis, -1), turn(ahead, axis, 1)]
        for axis, far, behind, ahead in (("z", kf, kn, km), ("x", vf, vn, vm))
    ]

    returning = sum_and_spread([t0, back_y, onward_y], back_ref)
    arrived = lax.all_to_all(returning, "seq", split_axis=0, concat_axis=0, tiled=True)
    neighbour_grad = settle(arrived, slot_reader, slot_live)

    done = [
        (mine + sum(v.astype(F32) for v in others))[0].T for mine, others in zip((k0, v0), came)
    ]
    return (query_grad, done[0], done[1], neighbour_grad)


def solution(mesh):
    placed = (
        P("seq", "tensor"),
        P("seq", "tensor"),
        P("seq", "tensor"),
        P(None, "tensor"),
        P(None, "tensor"),
        P(),
        P(),
        P(),
    )
    return jax.shard_map(
        local,
        mesh=mesh,
        in_specs=placed,
        out_specs=(P("seq", "tensor"), P("seq", "tensor"), P("seq", "tensor"), P("seq", "tensor")),
        check_vma=False,
    )
```

```python
import jax
import jax.numpy as jnp
from jax import lax
from jax.experimental import pallas as pl
from jax.experimental.pallas import tpu as pltpu
from jax.sharding import PartitionSpec as P

HEAD = 128
BLOCK = 64
NT = 128
NEIGH = 2
VMEM_LIMIT = 60 * 1024 * 1024
SMALL_LIMIT = 12 * 1024 * 1024
F32 = jnp.float32
BF16 = jnp.bfloat16


def params(limit=VMEM_LIMIT):
    return pltpu.CompilerParams(vmem_limit_bytes=limit)


def cost(flops, moved):
    return pl.CostEstimate(flops=flops // 1024, bytes_accessed=moved // 1024, transcendentals=0)


def dot(a, b, ca, cb):
    return lax.dot_general(a, b, (((ca,), (cb,)), ((), ())), preferred_element_type=F32)


ANY = pl.BlockSpec(memory_space=pl.ANY)
VMEM = pl.BlockSpec(memory_space=pltpu.VMEM)
SMEM = pl.BlockSpec(memory_space=pltpu.SMEM)


FAR, BACK, ON, OWN = 0, 1, 2, 3


def here():
    spot, column = lax.axis_index("seq"), lax.axis_index("tensor")
    return spot >> 2, spot & 3, column >> 1, column & 1


def moved(at, step):
    way = 1 - 2 * here()[3]
    return (at + (2, -way, way, 0)[step]) & 3


def piece_block(n):
    core = here()[3]
    step, other = ((OWN, 0), (OWN, 1), (BACK, 0), (ON, 1), (ON, 0), (BACK, 1), (FAR, 0), (FAR, 1))[n]
    return 2 * moved(here()[2], step) + (core ^ other)


def chunk_place(z, x):
    _, _, y, core = here()
    step, other = (z - y) & 3, (x >> 1) ^ core
    behind = step == moved(0, BACK)
    piece = jnp.where(
        step == 0,
        other,
        jnp.where(step == 2, 6 + other, jnp.where(behind, jnp.where(other == 1, 5, 2), jnp.where(other == 1, 3, 4))),
    )
    return 2 * piece + (x & 1)


def chunk_places(kind, step):
    z, x, _, _ = here()
    if kind == 0:
        return [chunk_place(moved(z, n), moved(x, step)) for n in range(4)]
    return [chunk_place(moved(z, step), moved(x, n)) for n in range(4)]


def spread(neighbours, send_slot, half):
    slots, rows, width = neighbours.shape
    count, part = send_slot.shape[0], rows // 2

    def body(s_ref, n_ref, o_ref, sems):
        copies = [
            pltpu.make_async_copy(
                n_ref.at[s_ref[p], pl.ds(half * part, part)], o_ref.at[p], sems.at[p]
            )
            for p in range(count)
        ]
        for copy in copies:
            copy.start()
        for copy in copies:
            copy.wait()

    return pl.pallas_call(
        body,
        in_specs=[SMEM, ANY],
        out_specs=VMEM,
        out_shape=jax.ShapeDtypeStruct((count, part, width), BF16),
        scratch_shapes=[pltpu.SemaphoreType.DMA((count,))],
        compiler_params=params(),
        cost_estimate=cost(0, 2 << 20),
        name="spread",
    )(send_slot, neighbours)


def pick(blocks, index):
    rows, width = blocks.shape[1:]
    count = index.shape[0]

    def body(i_ref, b_ref, o_ref, sems):
        copies = [
            pltpu.make_async_copy(b_ref.at[i_ref[n]], o_ref.at[pl.ds(n * rows, rows)], sems.at[n])
            for n in range(count)
        ]
        for copy in copies:
            copy.start()
        for copy in copies:
            copy.wait()

    return pl.pallas_call(
        body,
        in_specs=[SMEM, ANY],
        out_specs=VMEM,
        out_shape=jax.ShapeDtypeStruct((count * rows, width), BF16),
        scratch_shapes=[pltpu.SemaphoreType.DMA((count,))],
        compiler_params=params(SMALL_LIMIT),
        cost_estimate=cost(0, 2 << 20),
        name="pick",
    )(index, blocks)


def sum_and_spread(terms, index):
    parts, total, width = terms[0].shape
    rows = NT // 2
    count = index.shape[0]

    def body(i_ref, *refs):
        t_refs, (o_ref, held, sems) = refs[: len(terms)], refs[len(terms) :]
        copies = []
        for h in range(parts):
            held[h] = sum(r[h].astype(F32) for r in t_refs).astype(BF16)
            for p in range(count):
                source = held.at[h, pl.ds(pl.multiple_of(i_ref[p] * rows, rows), rows)]
                copies.append(
                    pltpu.make_async_copy(source, o_ref.at[p, pl.ds(h * rows, rows)], sems.at[h, p])
                )
                copies[-1].start()
        wait_all(copies)

    return pl.pallas_call(
        body,
        in_specs=[SMEM] + [VMEM] * len(terms),
        out_specs=ANY,
        out_shape=jax.ShapeDtypeStruct((count, parts * rows, width), BF16),
        scratch_shapes=[pltpu.VMEM((parts, total, width), BF16), pltpu.SemaphoreType.DMA((parts, count))],
        compiler_params=params(),
        cost_estimate=cost(0, 5 << 20),
        name="sum_and_spread",
    )(index, *terms)


def settle(arrived, index, live):
    rows, width = arrived.shape[1:]
    count = index.shape[0]

    def body(i_ref, l_ref, a_ref, o_ref, sems):
        def copy(n):
            return pltpu.make_async_copy(a_ref.at[i_ref[n]], o_ref.at[pl.ds(n * rows, rows)], sems.at[n])

        for n in range(count):
            pl.when(l_ref[n] > 0)(lambda n=n: copy(n).start())
        for n in range(count):

            @pl.when(l_ref[n] == 0)
            def _():
                o_ref[n * rows : (n + 1) * rows, :] = jnp.zeros((rows, width), BF16)

            pl.when(l_ref[n] > 0)(lambda n=n: copy(n).wait())

    return pl.pallas_call(
        body,
        in_specs=[SMEM] * 2 + [ANY],
        out_specs=VMEM,
        out_shape=jax.ShapeDtypeStruct((count * rows, width), BF16),
        scratch_shapes=[pltpu.SemaphoreType.DMA((count,))],
        compiler_params=params(SMALL_LIMIT),
        cost_estimate=cost(0, 2 << 20),
        name="settle",
    )(index, live, arrived)


def add_into(bases, extras):
    count = len(bases)

    def body(*refs):
        for n in range(count):
            b_ref, e_ref, o_ref = refs[n], refs[count + n], refs[2 * count + n]
            o_ref[...] = (b_ref[...].astype(F32) + e_ref[...].astype(F32)).astype(BF16)

    specs = [pl.BlockSpec((b.shape[0], b.shape[1] // 2, b.shape[2]), lambda i: (0, i, 0)) for b in bases]
    return pl.pallas_call(
        body,
        grid=(2,),
        in_specs=specs * 2,
        out_specs=specs,
        out_shape=[jax.ShapeDtypeStruct(b.shape, BF16) for b in bases],
        input_output_aliases={n: n for n in range(count)},
        compiler_params=params(),
        cost_estimate=cost(0, 2 * count << 20),
        name="add_into",
    )(*bases, *extras)


def read_in(sources, places, sems):
    copies = [pltpu.make_async_copy(a, b, sems.at[n]) for n, (a, b) in enumerate(zip(sources, places))]
    for copy in copies:
        copy.start()
    return copies


def wait_all(copies):
    for copy in copies:
        copy.wait()


def project_into(begin, piece_refs, k_ref, v_ref, all_ref, held, keys, values, acc, store, sems, out_sem):
    parts = len(piece_refs)
    rows, depth = piece_refs[0].shape
    width = k_ref.shape[1]
    waits = []
    for i in range(parts):
        span = pl.ds(i * depth, depth)
        source = pl.ds(pl.multiple_of(piece_block(i) * depth, depth), depth)
        waits.append(
            read_in(
                [piece_refs[i], k_ref.at[source], v_ref.at[source]],
                [held.at[:, span], keys.at[span], values.at[span]],
                sems.at[i],
            )
        )
    begun = begin()
    cuts = [0, parts // 2, parts]
    for lo, hi in zip(cuts[:-1], cuts[1:]):
        for i in range(lo, hi):
            wait_all(waits[i])
        span = slice(lo * depth, hi * depth)
        for n, w_ref in enumerate((keys, values)):
            cols = slice(n * width, (n + 1) * width)
            term = dot(held[:, span], w_ref[span, :], 1, 0)
            if lo == 0:
                acc[:, cols] = term
            else:
                store(cols, (acc[:, cols] + term).astype(BF16))
    chunk = all_ref.shape[2]
    outs = []
    for n in range(all_ref.shape[0]):
        outs.append(pltpu.make_async_copy(held.at[:, pl.ds(n * chunk, chunk)], all_ref.at[n], out_sem.at[n]))
        outs[-1].start()
    return begun, outs


def project_scratch(rows, parts, depth, width):
    return [
        pltpu.VMEM((rows, parts * depth), BF16),
        pltpu.VMEM((parts * depth, width), BF16),
        pltpu.VMEM((parts * depth, width), BF16),
        pltpu.VMEM((rows, 2 * width), F32),
        pltpu.SemaphoreType.DMA((parts, 3)),
        pltpu.SemaphoreType.DMA((parts * depth // 256,)),
    ]


def project(pieces, key_weight, value_weight):
    parts = len(pieces)
    rows, depth = pieces[0].shape
    width = key_weight.shape[1]

    def body(*refs):
        k_ref, v_ref, o_ref, all_ref, held, keys, values, acc, sems, out_sem = refs[parts:]

        def store(cols, value):
            o_ref[:, cols] = value

        _, last = project_into(
            lambda: None, refs[:parts], k_ref, v_ref, all_ref, held, keys, values, acc, store, sems, out_sem
        )
        wait_all(last)

    return pl.pallas_call(
        body,
        in_specs=[ANY] * (parts + 2),
        out_specs=[VMEM, ANY],
        out_shape=[
            jax.ShapeDtypeStruct((rows, 2 * width), BF16),
            jax.ShapeDtypeStruct((parts * depth // 256, rows, 256), BF16),
        ],
        scratch_shapes=project_scratch(rows, parts, depth, width),
        compiler_params=params(),
        cost_estimate=cost(4 * parts * rows * depth * width, 16 << 20),
        name="project",
    )(*pieces, key_weight, value_weight)


def project_attend(pieces, key_weight, value_weight, queries, out_grad, first_rows, lengths):
    parts = len(pieces)
    rows, depth = pieces[0].shape
    tokens, width = queries.shape
    blocks = tokens // BLOCK
    heads = width // HEAD
    span = NEIGH * NT
    part = span // 2
    sub = NT // 2
    scale = HEAD ** (-0.5)

    def body(len_ref, *refs):
        piece_refs, refs = refs[:parts], refs[parts:]
        k_ref, v_ref, q_in, g_in, a_in = refs[:5]
        all_ref, dq_out, p_out, t_out = refs[5:9]
        held, keys, values, acc, sems, out_sem = refs[9:15]
        q_ref, g_ref, a_ref, b_ref, dq_ref, p_ref, t_ref, in_sems, out_sems = refs[15:]

        def store(cols, value):
            b_ref[:, cols] = value

        def begin():
            return read_in([q_in, g_in, a_in], [q_ref, g_ref, a_ref], in_sems)

        early, last = project_into(
            begin, piece_refs, k_ref, v_ref, all_ref, held, keys, values, acc, store, sems, out_sem
        )
        wait_all(early)
        column = lax.broadcasted_iota(jnp.int32, (BLOCK, span), 1)
        row = (column // part) * sub + column % sub
        left = (column % part) < sub
        key_cols = [slice(h * HEAD, (h + 1) * HEAD) for h in range(heads)]
        value_cols = [slice(width + h * HEAD, width + (h + 1) * HEAD) for h in range(heads)]
        for block in range(blocks):
            mine = slice(block * BLOCK, (block + 1) * BLOCK)
            first = slice(block * part, (block + 1) * part)
            second = slice(rows + block * part, rows + (block + 1) * part)
            limit = jnp.where(left, len_ref[block * NEIGH], len_ref[block * NEIGH + 1])
            valid = row < limit
            both = lambda cols: jnp.concatenate([a_ref[first, cols], b_ref[first, cols]], axis=0)
            q = [q_ref[mine, c] for c in key_cols]
            g = [g_ref[mine, c] for c in key_cols]
            k = [both(c) for c in key_cols]
            v = [both(c) for c in value_cols]
            scores = [dot(q[h], k[h], 1, 1) for h in range(heads)]
            prob_grad = [dot(g[h], v[h], 1, 1) for h in range(heads)]
            attention = []
            for h in range(heads):
                masked = jnp.where(valid, scores[h] * scale, -jnp.inf)
                raised = jnp.exp(masked - jnp.max(masked, axis=1, keepdims=True))
                attention.append(raised / jnp.sum(raised, axis=1, keepdims=True))
            low = [a.astype(BF16) for a in attention]
            score_grad = []
            for h in range(heads):
                delta = jnp.sum(low[h].astype(F32) * prob_grad[h], axis=1, keepdims=True)
                score_grad.append((attention[h] * (prob_grad[h] - delta) * scale).astype(BF16))
            for h in range(heads):
                dq_ref[mine, key_cols[h]] = dot(score_grad[h], k[h], 1, 0).astype(BF16)
            for cols, lhs, rhs in ((key_cols, score_grad, q), (value_cols, low, g)):
                for h in range(heads):
                    grad = dot(lhs[h], rhs[h], 0, 0).astype(BF16)
                    p_ref[0, first, cols[h]] = grad[:part]
                    p_ref[1, first, cols[h]] = grad[part:]
                    grad_t = dot(rhs[h], lhs[h], 0, 0).astype(BF16)
                    t_ref[cols[h], first] = grad_t[:, :part]
                    t_ref[cols[h], second] = grad_t[:, part:]
        outs = read_in([p_ref, t_ref, dq_ref], [p_out, t_out, dq_out], out_sems)
        wait_all(outs)
        wait_all(last)

    shapes = [
        jax.ShapeDtypeStruct((parts * depth // 256, rows, 256), BF16),
        jax.ShapeDtypeStruct((tokens, width), BF16),
        jax.ShapeDtypeStruct((2, rows, 2 * width), BF16),
        jax.ShapeDtypeStruct((2 * width, 2 * rows), BF16),
    ]
    return pl.pallas_call(
        body,
        in_specs=[SMEM] + [ANY] * (parts + 5),
        out_specs=[ANY] * 4,
        out_shape=shapes,
        scratch_shapes=project_scratch(rows, parts, depth, width)
        + [pltpu.VMEM((tokens, width), BF16)] * 2
        + [pltpu.VMEM((rows, 2 * width), BF16)] * 2
        + [pltpu.VMEM(v.shape, BF16) for v in shapes[1:]]
        + [pltpu.SemaphoreType.DMA((3,))] * 2,
        compiler_params=params(),
        cost_estimate=cost(4 * parts * rows * depth * width, 16 << 20),
        name="project_attend",
    )(lengths, *pieces, key_weight, value_weight, queries, out_grad, first_rows)


def weight_groups(grads_t, rows, jobs, extras, name):
    chunk = 256
    both, count = grads_t.shape
    width, part, parts = both // 2, rows[0].shape[1], len(rows)
    chunks = 4 * len(jobs)
    shapes = [jax.ShapeDtypeStruct((4, width, chunk), BF16)] * len(jobs)

    def body(t_in, *refs):
        r_refs, e_refs = refs[:parts], refs[parts : parts + len(extras)]
        o_refs = refs[parts + len(extras) : parts + len(extras) + len(jobs)]
        t_ref, held, out_held, e_held, t_sem, r_sems, o_sems, e_sems = refs[parts + len(extras) + len(jobs) :]
        t_copy = pltpu.make_async_copy(t_in, t_ref, t_sem)
        t_copy.start()
        copies = []
        for n, place in enumerate([c for job in jobs for c in chunk_places(*job)]):
            copies.append(
                read_in(
                    [r.at[place] for r in r_refs],
                    [held.at[n, pl.ds(h * part, part)] for h in range(parts)],
                    r_sems.at[n],
                )
            )
        e_copies = read_in(e_refs, [e_held.at[n] for n in range(len(extras))], e_sems)
        t_copy.wait()
        outs, at = [], 0
        for job, (half, _) in enumerate(jobs):
            total = 4
            if job < 2:
                for copy in copies[:total] if job == 0 else copies[total:]:
                    wait_all(copy)
            if job == 0:
                wait_all(e_copies)
            for j in range(total):
                lhs = t_ref[half * width : (half + 1) * width, :]
                term = dot(lhs, held[at + j], 1, 0)
                if job < len(extras):
                    term = term + e_held[job, j].astype(F32)
                out_held[at + j] = term.astype(BF16)
            outs += read_in([out_held.at[pl.ds(at, total)]], [o_refs[job]], o_sems.at[pl.ds(job, 1)])
            at += total
        wait_all(outs)

    return pl.pallas_call(
        body,
        in_specs=[ANY] * (1 + parts + len(extras)),
        out_specs=[ANY] * len(jobs),
        out_shape=shapes,
        scratch_shapes=[
            pltpu.VMEM((both, count), BF16),
            pltpu.VMEM((chunks, count, chunk), BF16),
            pltpu.VMEM((chunks, width, chunk), BF16),
            pltpu.VMEM((max(len(extras), 1), 4, width, chunk), BF16),
            pltpu.SemaphoreType.DMA,
            pltpu.SemaphoreType.DMA((chunks, parts)),
            pltpu.SemaphoreType.DMA((len(jobs),)),
            pltpu.SemaphoreType.DMA((max(len(extras), 1),)),
        ],
        compiler_params=params(),
        cost_estimate=cost(2 * chunks * width * count * chunk, chunks * 3 << 18),
        name=name,
    )(grads_t, *rows, *extras)


def row_blocks(pairs, weights, steps, name):
    tile = 512
    halves, rows, both = pairs[0].shape
    width = both // 2
    count = len(steps)

    def body(*refs):
        p_in, w_in, o_refs = refs[:2], refs[2:6], refs[6 : 6 + count]
        p_ref, w_ref, o_held, p_sems, w_sems, o_sems = refs[6 + count :]
        p_copies = read_in(p_in, [p_ref.at[:, :, pl.ds(n * both, both)] for n in range(2)], p_sems)
        w_copies = []
        for n, step in enumerate(steps):
            chip = moved(here()[2], step)
            span = pl.ds(pl.multiple_of((2 * chip + here()[3]) * tile, tile), tile)
            sources = [w.at[span] for w in w_in]
            w_copies.append(
                read_in(sources, [w_ref.at[n, :, pl.ds(m * width, width)] for m in range(4)], w_sems.at[n])
            )
        wait_all(p_copies)
        outs = []
        for n in range(count):
            if n < 2:
                for copy in w_copies[:1] if n == 0 else w_copies[1:]:
                    wait_all(copy)
            for h in range(halves):
                o_held[n, h] = dot(p_ref[h], w_ref[n], 1, 1).astype(BF16)
            outs += read_in([o_held.at[n]], [o_refs[n]], o_sems.at[pl.ds(n, 1)])
        wait_all(outs)

    return pl.pallas_call(
        body,
        in_specs=[ANY] * 6,
        out_specs=[ANY] * count,
        out_shape=[jax.ShapeDtypeStruct((halves, rows, tile), BF16)] * count,
        scratch_shapes=[
            pltpu.VMEM((halves, rows, 2 * both), BF16),
            pltpu.VMEM((count, tile, 2 * both), BF16),
            pltpu.VMEM((count, halves, rows, tile), BF16),
            pltpu.SemaphoreType.DMA((2,)),
            pltpu.SemaphoreType.DMA((count, 4)),
            pltpu.SemaphoreType.DMA((count,)),
        ],
        compiler_params=params(),
        cost_estimate=cost(4 * count * halves * rows * tile * both, (2 + 2 * count) << 20),
        name=name,
    )(*pairs, *weights)


def turn(value, axis, sign):
    def to(i):
        z, x, y, core = i // 32, i // 8 % 4, i // 2 % 4, i % 2
        step = sign * (1 - 2 * core)
        if axis == "z":
            z = (z + step) % 4
        elif axis == "x":
            x = (x + step) % 4
        else:
            y = (y + step) % 4
        return ((z * 4 + x) * 4 + y) * 2 + core

    return lax.ppermute(value, ("seq", "tensor"), [(i, to(i)) for i in range(128)])


def jump(value, axis):
    to = lambda i: i ^ 8 if axis == "z" else i ^ 2
    return lax.ppermute(value, "seq", [(i, to(i)) for i in range(16)])


def swap(value):
    return lax.ppermute(value, "tensor", [(i, i ^ 1) for i in range(8)])


def after(value, *deps):
    return lax.optimization_barrier((value,) + deps)[0]


def ring_sums(own, first, second, name):
    _, width, chunk = own[0].shape

    def body(*refs):
        for n in range(2):
            ins, outs = refs[3 * n : 3 * n + 3], refs[6 + 4 * n : 10 + 4 * n]
            for j in range(4):
                value = sum(r[j].astype(F32) for r in ins)
                outs[j][...] = value if j == 3 else value.astype(BF16)

    whole = VMEM
    shapes = [jax.ShapeDtypeStruct((1, width, chunk), BF16)] * 3 + [jax.ShapeDtypeStruct((1, width, chunk), F32)]
    return pl.pallas_call(
        lambda *refs: body(*refs[:6], *[r.at[0] for r in refs[6:]]),
        in_specs=[whole] * 6,
        out_specs=[whole] * 8,
        out_shape=shapes * 2,
        compiler_params=params(),
        cost_estimate=cost(0, 10 << 20),
        name=name,
    )(own[0], first[0], second[0], own[1], first[1], second[1])


def gather_rows(own, last):
    near = turn(own, "y", 1)
    away = turn(own, "y", -1)
    far = turn(near, "y", 1)
    other = after(far, *last) if last else far
    return [own, swap(own), near, swap(near), away, swap(away), far, swap(other)], near


def local(queries, out_grad, neighbours, key_weight, value_weight, owner, slot, lengths):
    seq_count = lax.axis_size("seq")
    position = lax.axis_index("seq")
    core = here()[3]
    slot_count = lengths.shape[1]
    width = key_weight.shape[1]
    holders = owner.reshape(seq_count, -1)
    slots = slot.reshape(seq_count, -1)
    refs = holders.shape[1]
    order = jnp.arange(refs, dtype=jnp.int32)
    readers = jnp.arange(seq_count, dtype=jnp.int32)

    mine = holders == position
    send_slot = jnp.sum(jnp.where(mine, slots, 0), axis=1)
    my_holder = lax.dynamic_index_in_dim(holders, position, 0, keepdims=False)
    my_slot = lax.dynamic_index_in_dim(slots, position, 0, keepdims=False)
    my_lengths = jnp.take(lengths.reshape(-1), my_holder * slot_count + my_slot, mode="clip")
    back_ref = jnp.sum(jnp.where(my_holder[:, None] == readers[None, :], order[:, None], 0), axis=0)
    reads = mine[:, :, None] & (slots[:, :, None] == jnp.arange(slot_count, dtype=jnp.int32))
    slot_reader = jnp.sum(jnp.where(reads, readers[:, None, None], 0), axis=(0, 1))
    slot_live = jnp.any(reads, axis=(0, 1)).astype(jnp.int32)

    by_slot = neighbours.reshape(slot_count, NT, width)
    got_a = lax.all_to_all(spread(by_slot, send_slot, 0), "seq", split_axis=0, concat_axis=0, tiled=True)
    other_weights = [swap(key_weight), swap(value_weight)]
    send_b = after(spread(by_slot, send_slot, 1), got_a)
    got_b = lax.all_to_all(send_b, "seq", split_axis=0, concat_axis=0, tiled=True)
    rows_a, near_a = gather_rows(pick(got_a, my_holder), ())
    pair_a, all_a = project(rows_a, key_weight, value_weight)
    rows_b, _ = gather_rows(pick(after(got_b, near_a, my_lengths, *other_weights), my_holder), (pair_a,))
    all_b, query_grad, pair, pair_t = project_attend(
        rows_b, key_weight, value_weight, queries, out_grad, pair_a, my_lengths
    )

    def rows_of(earlier, steps, name):
        pairs = [after(pair, *earlier), other_pair] if earlier else [pair, other_pair]
        return row_blocks(pairs, [key_weight, value_weight] + other_weights, steps, name)

    other_pair = swap(pair)
    rows = [all_a, all_b]
    kf, vf, kn, vn = weight_groups(
        pair_t, rows, [(kind, step) for step in (FAR, BACK) for kind in (0, 1)], [], "weight_far"
    )
    far_x, far_z = turn(kf, "x", 1), turn(vf, "z", 1)
    (t2,) = rows_of((kf,), [FAR], "row_far")
    far_y = turn(t2, "y", 1)
    tn, tm, t0 = rows_of((t2,), [BACK, ON, OWN], "row_next")
    back_y = turn(tn, "y", -1)
    (tm,) = add_into([after(tm, tn, far_x, far_z)], [far_y])
    onward_y = turn(tm, "y", 1)
    back = [turn(after(kn, far_x, tm), "x", -1), turn(after(vn, far_z, tm), "z", -1)]
    km, vm, ko, vo = weight_groups(
        after(pair_t, tm),
        rows,
        [(kind, step) for step in (ON, OWN) for kind in (0, 1)],
        [far_x, far_z],
        "weight_rest",
    )
    km = after(km, back_y)
    km, vm = after(km, *back), after(vm, *back)
    onward = [turn(km, "x", 1), turn(vm, "z", 1)]

    kf, kn, km, k0, vf, vn, vm, v0 = ring_sums([ko, vo], back, onward, "ring_sums")
    came = [
        [jump(far, axis), turn(behind, axis, -1), turn(ahead, axis, 1)]
        for axis, far, behind, ahead in (("z", kf, kn, km), ("x", vf, vn, vm))
    ]

    returning = sum_and_spread([t0, back_y, onward_y], back_ref)
    arrived = lax.all_to_all(returning, "seq", split_axis=0, concat_axis=0, tiled=True)
    neighbour_grad = settle(arrived, slot_reader, slot_live)

    done = [
        (mine + sum(v.astype(F32) for v in others))[0].T for mine, others in zip((k0, v0), came)
    ]
    return (query_grad, done[0], done[1], neighbour_grad)


def solution(mesh):
    placed = (
        P("seq", "tensor"),
        P("seq", "tensor"),
        P("seq", "tensor"),
        P(None, "tensor"),
        P(None, "tensor"),
        P(),
        P(),
        P(),
    )
    return jax.shard_map(
        local,
        mesh=mesh,
        in_specs=placed,
        out_specs=(P("seq", "tensor"), P("seq", "tensor"), P("seq", "tensor"), P("seq", "tensor")),
        check_vma=False,
    )
```

```python
import jax
import jax.numpy as jnp
from jax import lax
from jax.experimental import pallas as pl
from jax.experimental.pallas import tpu as pltpu
from jax.sharding import PartitionSpec as P

HEAD = 128
BLOCK = 64
NT = 128
NEIGH = 2
VMEM_LIMIT = 60 * 1024 * 1024
SMALL_LIMIT = 12 * 1024 * 1024
F32 = jnp.float32
BF16 = jnp.bfloat16


def params(limit=VMEM_LIMIT):
    return pltpu.CompilerParams(vmem_limit_bytes=limit)


def cost(flops, moved):
    return pl.CostEstimate(flops=flops // 1024, bytes_accessed=moved // 1024, transcendentals=0)


def dot(a, b, ca, cb):
    return lax.dot_general(a, b, (((ca,), (cb,)), ((), ())), preferred_element_type=F32)


ANY = pl.BlockSpec(memory_space=pl.ANY)
VMEM = pl.BlockSpec(memory_space=pltpu.VMEM)
SMEM = pl.BlockSpec(memory_space=pltpu.SMEM)


FAR, BACK, ON, OWN = 0, 1, 2, 3


def here():
    spot, column = lax.axis_index("seq"), lax.axis_index("tensor")
    return spot >> 2, spot & 3, column >> 1, column & 1


def moved(at, step):
    way = 1 - 2 * here()[3]
    return (at + (2, -way, way, 0)[step]) & 3


def piece_block(n):
    core = here()[3]
    step, other = ((OWN, 0), (OWN, 1), (BACK, 0), (ON, 1), (ON, 0), (BACK, 1), (FAR, 0), (FAR, 1))[n]
    return 2 * moved(here()[2], step) + (core ^ other)


def chunk_place(z, x):
    _, _, y, core = here()
    step, other = (z - y) & 3, (x >> 1) ^ core
    behind = step == moved(0, BACK)
    piece = jnp.where(
        step == 0,
        other,
        jnp.where(step == 2, 6 + other, jnp.where(behind, jnp.where(other == 1, 5, 2), jnp.where(other == 1, 3, 4))),
    )
    return 2 * piece + (x & 1)


def chunk_places(kind, step):
    z, x, _, _ = here()
    if kind == 0:
        return [chunk_place(moved(z, n), moved(x, step)) for n in range(4)]
    return [chunk_place(moved(z, step), moved(x, n)) for n in range(4)]


def spread(neighbours, send_slot, half):
    slots, rows, width = neighbours.shape
    count, part = send_slot.shape[0], rows // 2

    def body(s_ref, n_ref, o_ref, sems):
        copies = [
            pltpu.make_async_copy(
                n_ref.at[s_ref[p], pl.ds(half * part, part)], o_ref.at[p], sems.at[p]
            )
            for p in range(count)
        ]
        for copy in copies:
            copy.start()
        for copy in copies:
            copy.wait()

    return pl.pallas_call(
        body,
        in_specs=[SMEM, ANY],
        out_specs=VMEM,
        out_shape=jax.ShapeDtypeStruct((count, part, width), BF16),
        scratch_shapes=[pltpu.SemaphoreType.DMA((count,))],
        compiler_params=params(),
        cost_estimate=cost(0, 2 << 20),
        name="spread",
    )(send_slot, neighbours)


def pick(blocks, index):
    rows, width = blocks.shape[1:]
    count = index.shape[0]

    def body(i_ref, b_ref, o_ref, sems):
        copies = [
            pltpu.make_async_copy(b_ref.at[i_ref[n]], o_ref.at[pl.ds(n * rows, rows)], sems.at[n])
            for n in range(count)
        ]
        for copy in copies:
            copy.start()
        for copy in copies:
            copy.wait()

    return pl.pallas_call(
        body,
        in_specs=[SMEM, ANY],
        out_specs=VMEM,
        out_shape=jax.ShapeDtypeStruct((count * rows, width), BF16),
        scratch_shapes=[pltpu.SemaphoreType.DMA((count,))],
        compiler_params=params(SMALL_LIMIT),
        cost_estimate=cost(0, 2 << 20),
        name="pick",
    )(index, blocks)


def sum_and_spread(terms, index):
    parts, total, width = terms[0].shape
    rows = NT // 2
    count = index.shape[0]

    def body(i_ref, *refs):
        t_refs, (o_ref, held, sems) = refs[: len(terms)], refs[len(terms) :]
        copies = []
        for h in range(parts):
            held[h] = sum(r[h].astype(F32) for r in t_refs).astype(BF16)
            for p in range(count):
                source = held.at[h, pl.ds(pl.multiple_of(i_ref[p] * rows, rows), rows)]
                copies.append(
                    pltpu.make_async_copy(source, o_ref.at[p, pl.ds(h * rows, rows)], sems.at[h, p])
                )
                copies[-1].start()
        wait_all(copies)

    return pl.pallas_call(
        body,
        in_specs=[SMEM] + [VMEM] * len(terms),
        out_specs=ANY,
        out_shape=jax.ShapeDtypeStruct((count, parts * rows, width), BF16),
        scratch_shapes=[pltpu.VMEM((parts, total, width), BF16), pltpu.SemaphoreType.DMA((parts, count))],
        compiler_params=params(),
        cost_estimate=cost(0, 5 << 20),
        name="sum_and_spread",
    )(index, *terms)


def settle(arrived, index, live):
    rows, width = arrived.shape[1:]
    count = index.shape[0]

    def body(i_ref, l_ref, a_ref, o_ref, sems):
        def copy(n):
            return pltpu.make_async_copy(a_ref.at[i_ref[n]], o_ref.at[pl.ds(n * rows, rows)], sems.at[n])

        for n in range(count):
            pl.when(l_ref[n] > 0)(lambda n=n: copy(n).start())
        for n in range(count):

            @pl.when(l_ref[n] == 0)
            def _():
                o_ref[n * rows : (n + 1) * rows, :] = jnp.zeros((rows, width), BF16)

            pl.when(l_ref[n] > 0)(lambda n=n: copy(n).wait())

    return pl.pallas_call(
        body,
        in_specs=[SMEM] * 2 + [ANY],
        out_specs=VMEM,
        out_shape=jax.ShapeDtypeStruct((count * rows, width), BF16),
        scratch_shapes=[pltpu.SemaphoreType.DMA((count,))],
        compiler_params=params(SMALL_LIMIT),
        cost_estimate=cost(0, 2 << 20),
        name="settle",
    )(index, live, arrived)


def add_into(bases, extras):
    count = len(bases)

    def body(*refs):
        for n in range(count):
            b_ref, e_ref, o_ref = refs[n], refs[count + n], refs[2 * count + n]
            o_ref[...] = (b_ref[...].astype(F32) + e_ref[...].astype(F32)).astype(BF16)

    specs = [pl.BlockSpec((b.shape[0], b.shape[1] // 2, b.shape[2]), lambda i: (0, i, 0)) for b in bases]
    return pl.pallas_call(
        body,
        grid=(2,),
        in_specs=specs * 2,
        out_specs=specs,
        out_shape=[jax.ShapeDtypeStruct(b.shape, BF16) for b in bases],
        input_output_aliases={n: n for n in range(count)},
        compiler_params=params(),
        cost_estimate=cost(0, 2 * count << 20),
        name="add_into",
    )(*bases, *extras)


def read_in(sources, places, sems):
    copies = [pltpu.make_async_copy(a, b, sems.at[n]) for n, (a, b) in enumerate(zip(sources, places))]
    for copy in copies:
        copy.start()
    return copies


def wait_all(copies):
    for copy in copies:
        copy.wait()


def project_into(begin, piece_refs, k_ref, v_ref, all_ref, held, keys, values, acc, store, sems, out_sem):
    parts = len(piece_refs)
    rows, depth = piece_refs[0].shape
    width = k_ref.shape[1]
    waits = []
    for i in range(parts):
        span = pl.ds(i * depth, depth)
        source = pl.ds(pl.multiple_of(piece_block(i) * depth, depth), depth)
        waits.append(
            read_in(
                [piece_refs[i], k_ref.at[source], v_ref.at[source]],
                [held.at[:, span], keys.at[span], values.at[span]],
                sems.at[i],
            )
        )
    begun = begin()
    cuts = [0, parts // 2, parts]
    for lo, hi in zip(cuts[:-1], cuts[1:]):
        for i in range(lo, hi):
            wait_all(waits[i])
        span = slice(lo * depth, hi * depth)
        for n, w_ref in enumerate((keys, values)):
            cols = slice(n * width, (n + 1) * width)
            term = dot(held[:, span], w_ref[span, :], 1, 0)
            if lo == 0:
                acc[:, cols] = term
            else:
                store(cols, (acc[:, cols] + term).astype(BF16))
    chunk = all_ref.shape[2]
    outs = []
    for n in range(all_ref.shape[0]):
        outs.append(pltpu.make_async_copy(held.at[:, pl.ds(n * chunk, chunk)], all_ref.at[n], out_sem.at[n]))
        outs[-1].start()
    return begun, outs


def project_scratch(rows, parts, depth, width):
    return [
        pltpu.VMEM((rows, parts * depth), BF16),
        pltpu.VMEM((parts * depth, width), BF16),
        pltpu.VMEM((parts * depth, width), BF16),
        pltpu.VMEM((rows, 2 * width), F32),
        pltpu.SemaphoreType.DMA((parts, 3)),
        pltpu.SemaphoreType.DMA((parts * depth // 256,)),
    ]


def project(pieces, key_weight, value_weight):
    parts = len(pieces)
    rows, depth = pieces[0].shape
    width = key_weight.shape[1]

    def body(*refs):
        k_ref, v_ref, o_ref, all_ref, held, keys, values, acc, sems, out_sem = refs[parts:]

        def store(cols, value):
            o_ref[:, cols] = value

        _, last = project_into(
            lambda: None, refs[:parts], k_ref, v_ref, all_ref, held, keys, values, acc, store, sems, out_sem
        )
        wait_all(last)

    return pl.pallas_call(
        body,
        in_specs=[ANY] * (parts + 2),
        out_specs=[VMEM, ANY],
        out_shape=[
            jax.ShapeDtypeStruct((rows, 2 * width), BF16),
            jax.ShapeDtypeStruct((parts * depth // 256, rows, 256), BF16),
        ],
        scratch_shapes=project_scratch(rows, parts, depth, width),
        compiler_params=params(),
        cost_estimate=cost(4 * parts * rows * depth * width, 16 << 20),
        name="project",
    )(*pieces, key_weight, value_weight)


def project_attend(pieces, key_weight, value_weight, queries, out_grad, first_rows, lengths):
    parts = len(pieces)
    rows, depth = pieces[0].shape
    tokens, width = queries.shape
    blocks = tokens // BLOCK
    heads = width // HEAD
    span = NEIGH * NT
    part = span // 2
    sub = NT // 2
    scale = HEAD ** (-0.5)

    def body(len_ref, *refs):
        piece_refs, refs = refs[:parts], refs[parts:]
        k_ref, v_ref, q_in, g_in, a_in = refs[:5]
        all_ref, dq_out, p_out, t_out = refs[5:9]
        held, keys, values, acc, sems, out_sem = refs[9:15]
        q_ref, g_ref, a_ref, b_ref, dq_ref, p_ref, t_ref, in_sems, out_sems = refs[15:]

        def store(cols, value):
            b_ref[:, cols] = value

        def begin():
            return read_in([q_in, g_in, a_in], [q_ref, g_ref, a_ref], in_sems)

        early, last = project_into(
            begin, piece_refs, k_ref, v_ref, all_ref, held, keys, values, acc, store, sems, out_sem
        )
        wait_all(early)
        column = lax.broadcasted_iota(jnp.int32, (BLOCK, span), 1)
        row = (column // part) * sub + column % sub
        left = (column % part) < sub
        key_cols = [slice(h * HEAD, (h + 1) * HEAD) for h in range(heads)]
        value_cols = [slice(width + h * HEAD, width + (h + 1) * HEAD) for h in range(heads)]
        outs = []
        for block in range(blocks):
            mine = slice(block * BLOCK, (block + 1) * BLOCK)
            first = slice(block * part, (block + 1) * part)
            second = slice(rows + block * part, rows + (block + 1) * part)
            limit = jnp.where(left, len_ref[block * NEIGH], len_ref[block * NEIGH + 1])
            valid = row < limit
            both = lambda cols: jnp.concatenate([a_ref[first, cols], b_ref[first, cols]], axis=0)
            q = [q_ref[mine, c] for c in key_cols]
            g = [g_ref[mine, c] for c in key_cols]
            k = [both(c) for c in key_cols]
            v = [both(c) for c in value_cols]
            scores = [dot(q[h], k[h], 1, 1) for h in range(heads)]
            prob_grad = [dot(g[h], v[h], 1, 1) for h in range(heads)]
            attention = []
            for h in range(heads):
                masked = jnp.where(valid, scores[h] * scale, -jnp.inf)
                raised = jnp.exp(masked - jnp.max(masked, axis=1, keepdims=True))
                attention.append(raised / jnp.sum(raised, axis=1, keepdims=True))
            low = [a.astype(BF16) for a in attention]
            score_grad = []
            for h in range(heads):
                delta = jnp.sum(low[h].astype(F32) * prob_grad[h], axis=1, keepdims=True)
                score_grad.append((attention[h] * (prob_grad[h] - delta) * scale).astype(BF16))
            for h in range(heads):
                dq_ref[mine, key_cols[h]] = dot(score_grad[h], k[h], 1, 0).astype(BF16)
            for cols, lhs, rhs in ((key_cols, score_grad, q), (value_cols, low, g)):
                for h in range(heads):
                    grad = dot(lhs[h], rhs[h], 0, 0).astype(BF16)
                    p_ref[0, first, cols[h]] = grad[:part]
                    p_ref[1, first, cols[h]] = grad[part:]
                    grad_t = dot(rhs[h], lhs[h], 0, 0).astype(BF16)
                    t_ref[cols[h], first] = grad_t[:, :part]
                    t_ref[cols[h], second] = grad_t[:, part:]
            outs += read_in(
                [p_ref.at[0, pl.ds(block * part, part)], p_ref.at[1, pl.ds(block * part, part)]],
                [p_out.at[0, pl.ds(block * part, part)], p_out.at[1, pl.ds(block * part, part)]],
                out_sems.at[pl.ds(2 * block, 2)],
            )
        outs += read_in([t_ref, dq_ref], [t_out, dq_out], out_sems.at[pl.ds(2 * blocks, 2)])
        wait_all(outs)
        wait_all(last)

    shapes = [
        jax.ShapeDtypeStruct((parts * depth // 256, rows, 256), BF16),
        jax.ShapeDtypeStruct((tokens, width), BF16),
        jax.ShapeDtypeStruct((2, rows, 2 * width), BF16),
        jax.ShapeDtypeStruct((2 * width, 2 * rows), BF16),
    ]
    return pl.pallas_call(
        body,
        in_specs=[SMEM] + [ANY] * (parts + 5),
        out_specs=[ANY] * 4,
        out_shape=shapes,
        scratch_shapes=project_scratch(rows, parts, depth, width)
        + [pltpu.VMEM((tokens, width), BF16)] * 2
        + [pltpu.VMEM((rows, 2 * width), BF16)] * 2
        + [pltpu.VMEM(v.shape, BF16) for v in shapes[1:]]
        + [pltpu.SemaphoreType.DMA((n,)) for n in (3, 2 * blocks + 2)],
        compiler_params=params(),
        cost_estimate=cost(4 * parts * rows * depth * width, 16 << 20),
        name="project_attend",
    )(lengths, *pieces, key_weight, value_weight, queries, out_grad, first_rows)


def weight_groups(grads_t, rows, jobs, extras, name):
    chunk = 256
    both, count = grads_t.shape
    width, part, parts = both // 2, rows[0].shape[1], len(rows)
    chunks = 4 * len(jobs)
    shapes = [jax.ShapeDtypeStruct((4, width, chunk), BF16)] * len(jobs)

    def body(t_in, *refs):
        r_refs, e_refs = refs[:parts], refs[parts : parts + len(extras)]
        o_refs = refs[parts + len(extras) : parts + len(extras) + len(jobs)]
        t_ref, held, out_held, e_held, t_sem, r_sems, o_sems, e_sems = refs[parts + len(extras) + len(jobs) :]
        t_copy = pltpu.make_async_copy(t_in, t_ref, t_sem)
        t_copy.start()
        copies = []
        for n, place in enumerate([c for job in jobs for c in chunk_places(*job)]):
            copies.append(
                read_in(
                    [r.at[place] for r in r_refs],
                    [held.at[n, pl.ds(h * part, part)] for h in range(parts)],
                    r_sems.at[n],
                )
            )
        e_copies = read_in(e_refs, [e_held.at[n] for n in range(len(extras))], e_sems)
        t_copy.wait()
        outs, at = [], 0
        for job, (half, _) in enumerate(jobs):
            total = 4
            if job < 2:
                for copy in copies[:total] if job == 0 else copies[total:]:
                    wait_all(copy)
            if job == 0:
                wait_all(e_copies)
            for j in range(total):
                lhs = t_ref[half * width : (half + 1) * width, :]
                term = dot(lhs, held[at + j], 1, 0)
                if job < len(extras):
                    term = term + e_held[job, j].astype(F32)
                out_held[at + j] = term.astype(BF16)
            outs += read_in([out_held.at[pl.ds(at, total)]], [o_refs[job]], o_sems.at[pl.ds(job, 1)])
            at += total
        wait_all(outs)

    return pl.pallas_call(
        body,
        in_specs=[ANY] * (1 + parts + len(extras)),
        out_specs=[ANY] * len(jobs),
        out_shape=shapes,
        scratch_shapes=[
            pltpu.VMEM((both, count), BF16),
            pltpu.VMEM((chunks, count, chunk), BF16),
            pltpu.VMEM((chunks, width, chunk), BF16),
            pltpu.VMEM((max(len(extras), 1), 4, width, chunk), BF16),
            pltpu.SemaphoreType.DMA,
            pltpu.SemaphoreType.DMA((chunks, parts)),
            pltpu.SemaphoreType.DMA((len(jobs),)),
            pltpu.SemaphoreType.DMA((max(len(extras), 1),)),
        ],
        compiler_params=params(),
        cost_estimate=cost(2 * chunks * width * count * chunk, chunks * 3 << 18),
        name=name,
    )(grads_t, *rows, *extras)


def row_blocks(pairs, weights, steps, name):
    tile = 512
    halves, rows, both = pairs[0].shape
    width = both // 2
    count = len(steps)

    def body(*refs):
        p_in, w_in, o_refs = refs[:2], refs[2:6], refs[6 : 6 + count]
        p_ref, w_ref, o_held, p_sems, w_sems, o_sems = refs[6 + count :]
        p_copies = read_in(p_in, [p_ref.at[:, :, pl.ds(n * both, both)] for n in range(2)], p_sems)
        w_copies = []
        for n, step in enumerate(steps):
            chip = moved(here()[2], step)
            span = pl.ds(pl.multiple_of((2 * chip + here()[3]) * tile, tile), tile)
            sources = [w.at[span] for w in w_in]
            w_copies.append(
                read_in(sources, [w_ref.at[n, :, pl.ds(m * width, width)] for m in range(4)], w_sems.at[n])
            )
        wait_all(p_copies)
        outs = []
        for n in range(count):
            if n < 2:
                for copy in w_copies[:1] if n == 0 else w_copies[1:]:
                    wait_all(copy)
            for h in range(halves):
                o_held[n, h] = dot(p_ref[h], w_ref[n], 1, 1).astype(BF16)
            outs += read_in([o_held.at[n]], [o_refs[n]], o_sems.at[pl.ds(n, 1)])
        wait_all(outs)

    return pl.pallas_call(
        body,
        in_specs=[ANY] * 6,
        out_specs=[ANY] * count,
        out_shape=[jax.ShapeDtypeStruct((halves, rows, tile), BF16)] * count,
        scratch_shapes=[
            pltpu.VMEM((halves, rows, 2 * both), BF16),
            pltpu.VMEM((count, tile, 2 * both), BF16),
            pltpu.VMEM((count, halves, rows, tile), BF16),
            pltpu.SemaphoreType.DMA((2,)),
            pltpu.SemaphoreType.DMA((count, 4)),
            pltpu.SemaphoreType.DMA((count,)),
        ],
        compiler_params=params(),
        cost_estimate=cost(4 * count * halves * rows * tile * both, (2 + 2 * count) << 20),
        name=name,
    )(*pairs, *weights)


def turn(value, axis, sign):
    def to(i):
        z, x, y, core = i // 32, i // 8 % 4, i // 2 % 4, i % 2
        step = sign * (1 - 2 * core)
        if axis == "z":
            z = (z + step) % 4
        elif axis == "x":
            x = (x + step) % 4
        else:
            y = (y + step) % 4
        return ((z * 4 + x) * 4 + y) * 2 + core

    return lax.ppermute(value, ("seq", "tensor"), [(i, to(i)) for i in range(128)])


def jump(value, axis):
    to = lambda i: i ^ 8 if axis == "z" else i ^ 2
    return lax.ppermute(value, "seq", [(i, to(i)) for i in range(16)])


def swap(value):
    return lax.ppermute(value, "tensor", [(i, i ^ 1) for i in range(8)])


def after(value, *deps):
    return lax.optimization_barrier((value,) + deps)[0]


def ring_sums(own, first, second, name):
    _, width, chunk = own[0].shape

    def body(*refs):
        for n in range(2):
            ins, outs = refs[3 * n : 3 * n + 3], refs[6 + 4 * n : 10 + 4 * n]
            for j in range(4):
                value = sum(r[j].astype(F32) for r in ins)
                outs[j][...] = value if j == 3 else value.astype(BF16)

    whole = VMEM
    shapes = [jax.ShapeDtypeStruct((1, width, chunk), BF16)] * 3 + [jax.ShapeDtypeStruct((1, width, chunk), F32)]
    return pl.pallas_call(
        lambda *refs: body(*refs[:6], *[r.at[0] for r in refs[6:]]),
        in_specs=[whole] * 6,
        out_specs=[whole] * 8,
        out_shape=shapes * 2,
        compiler_params=params(),
        cost_estimate=cost(0, 10 << 20),
        name=name,
    )(own[0], first[0], second[0], own[1], first[1], second[1])


def gather_rows(own, last):
    near = turn(own, "y", 1)
    away = turn(own, "y", -1)
    far = turn(near, "y", 1)
    other = after(far, *last) if last else far
    return [own, swap(own), near, swap(near), away, swap(away), far, swap(other)], near


def local(queries, out_grad, neighbours, key_weight, value_weight, owner, slot, lengths):
    seq_count = lax.axis_size("seq")
    position = lax.axis_index("seq")
    core = here()[3]
    slot_count = lengths.shape[1]
    width = key_weight.shape[1]
    holders = owner.reshape(seq_count, -1)
    slots = slot.reshape(seq_count, -1)
    refs = holders.shape[1]
    order = jnp.arange(refs, dtype=jnp.int32)
    readers = jnp.arange(seq_count, dtype=jnp.int32)

    mine = holders == position
    send_slot = jnp.sum(jnp.where(mine, slots, 0), axis=1)
    my_holder = lax.dynamic_index_in_dim(holders, position, 0, keepdims=False)
    my_slot = lax.dynamic_index_in_dim(slots, position, 0, keepdims=False)
    my_lengths = jnp.take(lengths.reshape(-1), my_holder * slot_count + my_slot, mode="clip")
    back_ref = jnp.sum(jnp.where(my_holder[:, None] == readers[None, :], order[:, None], 0), axis=0)
    reads = mine[:, :, None] & (slots[:, :, None] == jnp.arange(slot_count, dtype=jnp.int32))
    slot_reader = jnp.sum(jnp.where(reads, readers[:, None, None], 0), axis=(0, 1))
    slot_live = jnp.any(reads, axis=(0, 1)).astype(jnp.int32)

    by_slot = neighbours.reshape(slot_count, NT, width)
    got_a = lax.all_to_all(spread(by_slot, send_slot, 0), "seq", split_axis=0, concat_axis=0, tiled=True)
    other_weights = [swap(key_weight), swap(value_weight)]
    send_b = after(spread(by_slot, send_slot, 1), got_a)
    got_b = lax.all_to_all(send_b, "seq", split_axis=0, concat_axis=0, tiled=True)
    rows_a, near_a = gather_rows(pick(got_a, my_holder), ())
    pair_a, all_a = project(rows_a, key_weight, value_weight)
    rows_b, _ = gather_rows(pick(after(got_b, near_a, my_lengths, *other_weights), my_holder), (pair_a,))
    all_b, query_grad, pair, pair_t = project_attend(
        rows_b, key_weight, value_weight, queries, out_grad, pair_a, my_lengths
    )

    def rows_of(earlier, steps, name):
        pairs = [after(pair, *earlier), other_pair] if earlier else [pair, other_pair]
        return row_blocks(pairs, [key_weight, value_weight] + other_weights, steps, name)

    other_pair = swap(pair)
    rows = [all_a, all_b]
    kf, vf, kn, vn = weight_groups(
        pair_t, rows, [(kind, step) for step in (FAR, BACK) for kind in (0, 1)], [], "weight_far"
    )
    (t2,) = rows_of((kf,), [FAR], "row_far")
    far_x, far_z = turn(after(kf, t2), "x", 1), turn(after(vf, t2), "z", 1)
    far_y = turn(t2, "y", 1)
    tn, tm, t0 = rows_of((t2,), [BACK, ON, OWN], "row_next")
    back_y = turn(tn, "y", -1)
    (tm,) = add_into([after(tm, tn)], [far_y])
    onward_y = turn(tm, "y", 1)
    back = [turn(after(kn, far_x, tm), "x", -1), turn(after(vn, far_z, tm), "z", -1)]
    km, vm, ko, vo = weight_groups(
        after(pair_t, tm),
        rows,
        [(kind, step) for step in (ON, OWN) for kind in (0, 1)],
        [far_x, far_z],
        "weight_rest",
    )
    km = after(km, back_y)
    km, vm = after(km, *back), after(vm, *back)
    onward = [turn(km, "x", 1), turn(vm, "z", 1)]

    kf, kn, km, k0, vf, vn, vm, v0 = ring_sums([ko, vo], back, onward, "ring_sums")
    came = [
        [jump(far, axis), turn(behind, axis, -1), turn(ahead, axis, 1)]
        for axis, far, behind, ahead in (("z", kf, kn, km), ("x", vf, vn, vm))
    ]

    returning = sum_and_spread([t0, back_y, onward_y], back_ref)
    arrived = lax.all_to_all(returning, "seq", split_axis=0, concat_axis=0, tiled=True)
    neighbour_grad = settle(arrived, slot_reader, slot_live)

    done = [
        (mine + sum(v.astype(F32) for v in others))[0].T for mine, others in zip((k0, v0), came)
    ]
    return (query_grad, done[0], done[1], neighbour_grad)


def solution(mesh):
    placed = (
        P("seq", "tensor"),
        P("seq", "tensor"),
        P("seq", "tensor"),
        P(None, "tensor"),
        P(None, "tensor"),
        P(),
        P(),
        P(),
    )
    return jax.shard_map(
        local,
        mesh=mesh,
        in_specs=placed,
        out_specs=(P("seq", "tensor"), P("seq", "tensor"), P("seq", "tensor"), P("seq", "tensor")),
        check_vma=False,
    )
```

```python
import jax
import jax.numpy as jnp
from jax import lax
from jax.experimental import pallas as pl
from jax.experimental.pallas import tpu as pltpu
from jax.sharding import PartitionSpec as P

HEAD = 128
BLOCK = 64
NT = 128
NEIGH = 2
VMEM_LIMIT = 60 * 1024 * 1024
SMALL_LIMIT = 12 * 1024 * 1024
F32 = jnp.float32
BF16 = jnp.bfloat16


def params(limit=VMEM_LIMIT):
    return pltpu.CompilerParams(vmem_limit_bytes=limit)


def cost(flops, moved):
    return pl.CostEstimate(flops=flops // 1024, bytes_accessed=moved // 1024, transcendentals=0)


def dot(a, b, ca, cb):
    return lax.dot_general(a, b, (((ca,), (cb,)), ((), ())), preferred_element_type=F32)


ANY = pl.BlockSpec(memory_space=pl.ANY)
VMEM = pl.BlockSpec(memory_space=pltpu.VMEM)
SMEM = pl.BlockSpec(memory_space=pltpu.SMEM)


FAR, BACK, ON, OWN = 0, 1, 2, 3


def here():
    spot, column = lax.axis_index("seq"), lax.axis_index("tensor")
    return spot >> 2, spot & 3, column >> 1, column & 1


def moved(at, step):
    way = 1 - 2 * here()[3]
    return (at + (2, -way, way, 0)[step]) & 3


def piece_block(n):
    core = here()[3]
    step, other = ((OWN, 0), (OWN, 1), (BACK, 0), (ON, 1), (ON, 0), (BACK, 1), (FAR, 0), (FAR, 1))[n]
    return 2 * moved(here()[2], step) + (core ^ other)


def chunk_place(z, x):
    _, _, y, core = here()
    step, other = (z - y) & 3, (x >> 1) ^ core
    behind = step == moved(0, BACK)
    piece = jnp.where(
        step == 0,
        other,
        jnp.where(step == 2, 6 + other, jnp.where(behind, jnp.where(other == 1, 5, 2), jnp.where(other == 1, 3, 4))),
    )
    return 2 * piece + (x & 1)


def chunk_places(kind, step):
    z, x, _, _ = here()
    if kind == 0:
        return [chunk_place(moved(z, n), moved(x, step)) for n in range(4)]
    return [chunk_place(moved(z, step), moved(x, n)) for n in range(4)]


def spread(neighbours, send_slot, half):
    slots, rows, width = neighbours.shape
    count, part = send_slot.shape[0], rows // 2

    def body(s_ref, n_ref, o_ref, sems):
        copies = [
            pltpu.make_async_copy(
                n_ref.at[s_ref[p], pl.ds(half * part, part)], o_ref.at[p], sems.at[p]
            )
            for p in range(count)
        ]
        for copy in copies:
            copy.start()
        for copy in copies:
            copy.wait()

    return pl.pallas_call(
        body,
        in_specs=[SMEM, ANY],
        out_specs=VMEM,
        out_shape=jax.ShapeDtypeStruct((count, part, width), BF16),
        scratch_shapes=[pltpu.SemaphoreType.DMA((count,))],
        compiler_params=params(),
        cost_estimate=cost(0, 2 << 20),
        name="spread",
    )(send_slot, neighbours)


def pick(blocks, index):
    rows, width = blocks.shape[1:]
    count = index.shape[0]

    def body(i_ref, b_ref, o_ref, sems):
        copies = [
            pltpu.make_async_copy(b_ref.at[i_ref[n]], o_ref.at[pl.ds(n * rows, rows)], sems.at[n])
            for n in range(count)
        ]
        for copy in copies:
            copy.start()
        for copy in copies:
            copy.wait()

    return pl.pallas_call(
        body,
        in_specs=[SMEM, ANY],
        out_specs=VMEM,
        out_shape=jax.ShapeDtypeStruct((count * rows, width), BF16),
        scratch_shapes=[pltpu.SemaphoreType.DMA((count,))],
        compiler_params=params(SMALL_LIMIT),
        cost_estimate=cost(0, 2 << 20),
        name="pick",
    )(index, blocks)


def sum_and_spread(terms, index):
    parts, total, width = terms[0].shape
    rows = NT // 2
    count = index.shape[0]

    def body(i_ref, *refs):
        t_refs, (o_ref, held, parts_held, sems, in_sems) = refs[: len(terms)], refs[len(terms) :]
        came = [
            read_in([r.at[h] for r in t_refs], [parts_held.at[h, n] for n in range(len(terms))], in_sems.at[h])
            for h in range(parts)
        ]
        copies = []
        for h in range(parts):
            wait_all(came[h])
            held[h] = sum(parts_held[h, n].astype(F32) for n in range(len(terms))).astype(BF16)
            for p in range(count):
                source = held.at[h, pl.ds(pl.multiple_of(i_ref[p] * rows, rows), rows)]
                copies.append(
                    pltpu.make_async_copy(source, o_ref.at[p, pl.ds(h * rows, rows)], sems.at[h, p])
                )
                copies[-1].start()
        wait_all(copies)

    return pl.pallas_call(
        body,
        in_specs=[SMEM] + [ANY] * len(terms),
        out_specs=ANY,
        out_shape=jax.ShapeDtypeStruct((count, parts * rows, width), BF16),
        scratch_shapes=[
            pltpu.VMEM((parts, total, width), BF16),
            pltpu.VMEM((parts, len(terms), total, width), BF16),
            pltpu.SemaphoreType.DMA((parts, count)),
            pltpu.SemaphoreType.DMA((parts, len(terms))),
        ],
        compiler_params=params(),
        cost_estimate=cost(0, 5 << 20),
        name="sum_and_spread",
    )(index, *terms)


def settle(arrived, index, live):
    rows, width = arrived.shape[1:]
    count = index.shape[0]

    def body(i_ref, l_ref, a_ref, o_ref, sems):
        def copy(n):
            return pltpu.make_async_copy(a_ref.at[i_ref[n]], o_ref.at[pl.ds(n * rows, rows)], sems.at[n])

        for n in range(count):
            pl.when(l_ref[n] > 0)(lambda n=n: copy(n).start())
        for n in range(count):

            @pl.when(l_ref[n] == 0)
            def _():
                o_ref[n * rows : (n + 1) * rows, :] = jnp.zeros((rows, width), BF16)

            pl.when(l_ref[n] > 0)(lambda n=n: copy(n).wait())

    return pl.pallas_call(
        body,
        in_specs=[SMEM] * 2 + [ANY],
        out_specs=VMEM,
        out_shape=jax.ShapeDtypeStruct((count * rows, width), BF16),
        scratch_shapes=[pltpu.SemaphoreType.DMA((count,))],
        compiler_params=params(SMALL_LIMIT),
        cost_estimate=cost(0, 2 << 20),
        name="settle",
    )(index, live, arrived)


def add_into(bases, extras):
    count = len(bases)

    def body(*refs):
        for n in range(count):
            b_ref, e_ref, o_ref = refs[n], refs[count + n], refs[2 * count + n]
            o_ref[...] = (b_ref[...].astype(F32) + e_ref[...].astype(F32)).astype(BF16)

    specs = [pl.BlockSpec((b.shape[0], b.shape[1] // 2, b.shape[2]), lambda i: (0, i, 0)) for b in bases]
    return pl.pallas_call(
        body,
        grid=(2,),
        in_specs=specs * 2,
        out_specs=specs,
        out_shape=[jax.ShapeDtypeStruct(b.shape, BF16) for b in bases],
        input_output_aliases={n: n for n in range(count)},
        compiler_params=params(),
        cost_estimate=cost(0, 2 * count << 20),
        name="add_into",
    )(*bases, *extras)


def read_in(sources, places, sems):
    copies = [pltpu.make_async_copy(a, b, sems.at[n]) for n, (a, b) in enumerate(zip(sources, places))]
    for copy in copies:
        copy.start()
    return copies


def wait_all(copies):
    for copy in copies:
        copy.wait()


def project_into(begin, piece_refs, k_ref, v_ref, all_ref, held, keys, values, acc, store, sems, out_sem):
    parts = len(piece_refs)
    rows, depth = piece_refs[0].shape
    width = k_ref.shape[1]
    waits = []
    for i in range(parts):
        span = pl.ds(i * depth, depth)
        source = pl.ds(pl.multiple_of(piece_block(i) * depth, depth), depth)
        waits.append(
            read_in(
                [piece_refs[i], k_ref.at[source], v_ref.at[source]],
                [held.at[:, span], keys.at[span], values.at[span]],
                sems.at[i],
            )
        )
    begun = begin()
    cuts = [0, parts // 4, 5 * parts // 8, parts]
    for lo, hi in zip(cuts[:-1], cuts[1:]):
        for i in range(lo, hi):
            wait_all(waits[i])
        span = slice(lo * depth, hi * depth)
        for n, w_ref in enumerate((keys, values)):
            cols = slice(n * width, (n + 1) * width)
            term = dot(held[:, span], w_ref[span, :], 1, 0)
            if lo == 0:
                acc[:, cols] = term
            elif hi < parts:
                acc[:, cols] += term
            else:
                store(cols, (acc[:, cols] + term).astype(BF16))
    chunk = all_ref.shape[2]
    outs = []
    for n in range(all_ref.shape[0]):
        outs.append(pltpu.make_async_copy(held.at[:, pl.ds(n * chunk, chunk)], all_ref.at[n], out_sem.at[n]))
        outs[-1].start()
    return begun, outs


def project_scratch(rows, parts, depth, width):
    return [
        pltpu.VMEM((rows, parts * depth), BF16),
        pltpu.VMEM((parts * depth, width), BF16),
        pltpu.VMEM((parts * depth, width), BF16),
        pltpu.VMEM((rows, 2 * width), F32),
        pltpu.SemaphoreType.DMA((parts, 3)),
        pltpu.SemaphoreType.DMA((parts * depth // 256,)),
    ]


def project(pieces, key_weight, value_weight):
    parts = len(pieces)
    rows, depth = pieces[0].shape
    width = key_weight.shape[1]

    def body(*refs):
        k_ref, v_ref, o_ref, all_ref, held, keys, values, acc, sems, out_sem = refs[parts:]

        def store(cols, value):
            o_ref[:, cols] = value

        _, last = project_into(
            lambda: None, refs[:parts], k_ref, v_ref, all_ref, held, keys, values, acc, store, sems, out_sem
        )
        wait_all(last)

    return pl.pallas_call(
        body,
        in_specs=[ANY] * (parts + 2),
        out_specs=[VMEM, ANY],
        out_shape=[
            jax.ShapeDtypeStruct((rows, 2 * width), BF16),
            jax.ShapeDtypeStruct((parts * depth // 256, rows, 256), BF16),
        ],
        scratch_shapes=project_scratch(rows, parts, depth, width),
        compiler_params=params(),
        cost_estimate=cost(4 * parts * rows * depth * width, 16 << 20),
        name="project",
    )(*pieces, key_weight, value_weight)


def project_attend(pieces, key_weight, value_weight, queries, out_grad, first_rows, lengths):
    parts = len(pieces)
    rows, depth = pieces[0].shape
    tokens, width = queries.shape
    blocks = tokens // BLOCK
    heads = width // HEAD
    span = NEIGH * NT
    part = span // 2
    sub = NT // 2
    scale = HEAD ** (-0.5)

    def body(len_ref, *refs):
        piece_refs, refs = refs[:parts], refs[parts:]
        k_ref, v_ref, q_in, g_in, a_in = refs[:5]
        all_ref, dq_out, p_out, t_out = refs[5:9]
        held, keys, values, acc, sems, out_sem = refs[9:15]
        q_ref, g_ref, a_ref, b_ref, dq_ref, p_ref, t_ref, in_sems, out_sems = refs[15:]

        def store(cols, value):
            b_ref[:, cols] = value

        def begin():
            return read_in([q_in, g_in, a_in], [q_ref, g_ref, a_ref], in_sems)

        early, last = project_into(
            begin, piece_refs, k_ref, v_ref, all_ref, held, keys, values, acc, store, sems, out_sem
        )
        wait_all(early)
        column = lax.broadcasted_iota(jnp.int32, (BLOCK, span), 1)
        row = (column // part) * sub + column % sub
        left = (column % part) < sub
        key_cols = [slice(h * HEAD, (h + 1) * HEAD) for h in range(heads)]
        value_cols = [slice(width + h * HEAD, width + (h + 1) * HEAD) for h in range(heads)]
        outs = []
        for block in range(blocks):
            mine = slice(block * BLOCK, (block + 1) * BLOCK)
            first = slice(block * part, (block + 1) * part)
            second = slice(rows + block * part, rows + (block + 1) * part)
            limit = jnp.where(left, len_ref[block * NEIGH], len_ref[block * NEIGH + 1])
            valid = row < limit
            both = lambda cols: jnp.concatenate([a_ref[first, cols], b_ref[first, cols]], axis=0)
            q = [q_ref[mine, c] for c in key_cols]
            g = [g_ref[mine, c] for c in key_cols]
            k = [both(c) for c in key_cols]
            v = [both(c) for c in value_cols]
            scores = [dot(q[h], k[h], 1, 1) for h in range(heads)]
            prob_grad = [dot(g[h], v[h], 1, 1) for h in range(heads)]
            attention = []
            for h in range(heads):
                masked = jnp.where(valid, scores[h] * scale, -jnp.inf)
                raised = jnp.exp(masked - jnp.max(masked, axis=1, keepdims=True))
                attention.append(raised / jnp.sum(raised, axis=1, keepdims=True))
            low = [a.astype(BF16) for a in attention]
            score_grad = []
            for h in range(heads):
                delta = jnp.sum(low[h].astype(F32) * prob_grad[h], axis=1, keepdims=True)
                score_grad.append((attention[h] * (prob_grad[h] - delta) * scale).astype(BF16))
            for h in range(heads):
                dq_ref[mine, key_cols[h]] = dot(score_grad[h], k[h], 1, 0).astype(BF16)
            for cols, lhs, rhs in ((key_cols, score_grad, q), (value_cols, low, g)):
                for h in range(heads):
                    grad = dot(lhs[h], rhs[h], 0, 0).astype(BF16)
                    p_ref[0, first, cols[h]] = grad[:part]
                    p_ref[1, first, cols[h]] = grad[part:]
                    grad_t = dot(rhs[h], lhs[h], 0, 0).astype(BF16)
                    t_ref[cols[h], first] = grad_t[:, :part]
                    t_ref[cols[h], second] = grad_t[:, part:]
            outs += read_in(
                [p_ref.at[0, pl.ds(block * part, part)], p_ref.at[1, pl.ds(block * part, part)]],
                [p_out.at[0, pl.ds(block * part, part)], p_out.at[1, pl.ds(block * part, part)]],
                out_sems.at[pl.ds(2 * block, 2)],
            )
        outs += read_in([t_ref, dq_ref], [t_out, dq_out], out_sems.at[pl.ds(2 * blocks, 2)])
        wait_all(outs)
        wait_all(last)

    shapes = [
        jax.ShapeDtypeStruct((parts * depth // 256, rows, 256), BF16),
        jax.ShapeDtypeStruct((tokens, width), BF16),
        jax.ShapeDtypeStruct((2, rows, 2 * width), BF16),
        jax.ShapeDtypeStruct((2 * width, 2 * rows), BF16),
    ]
    return pl.pallas_call(
        body,
        in_specs=[SMEM] + [ANY] * (parts + 5),
        out_specs=[ANY] * 4,
        out_shape=shapes,
        scratch_shapes=project_scratch(rows, parts, depth, width)
        + [pltpu.VMEM((tokens, width), BF16)] * 2
        + [pltpu.VMEM((rows, 2 * width), BF16)] * 2
        + [pltpu.VMEM(v.shape, BF16) for v in shapes[1:]]
        + [pltpu.SemaphoreType.DMA((n,)) for n in (3, 2 * blocks + 2)],
        compiler_params=params(),
        cost_estimate=cost(4 * parts * rows * depth * width, 16 << 20),
        name="project_attend",
    )(lengths, *pieces, key_weight, value_weight, queries, out_grad, first_rows)


def weight_groups(grads_t, rows, jobs, extras, name):
    chunk = 256
    both, count = grads_t.shape
    width, part, parts = both // 2, rows[0].shape[1], len(rows)
    chunks = 4 * len(jobs)
    shapes = [jax.ShapeDtypeStruct((4, width, chunk), BF16)] * len(jobs)

    def body(t_in, *refs):
        r_refs, e_refs = refs[:parts], refs[parts : parts + len(extras)]
        o_refs = refs[parts + len(extras) : parts + len(extras) + len(jobs)]
        t_ref, held, out_held, e_held, t_sem, r_sems, o_sems, e_sems = refs[parts + len(extras) + len(jobs) :]
        t_copy = pltpu.make_async_copy(t_in, t_ref, t_sem)
        t_copy.start()
        copies = []
        for n, place in enumerate([c for job in jobs for c in chunk_places(*job)]):
            copies.append(
                read_in(
                    [r.at[place] for r in r_refs],
                    [held.at[n, pl.ds(h * part, part)] for h in range(parts)],
                    r_sems.at[n],
                )
            )
        e_copies = read_in(e_refs, [e_held.at[n] for n in range(len(extras))], e_sems)
        t_copy.wait()
        outs, at = [], 0
        for job, (half, _) in enumerate(jobs):
            total = 4
            if job < 2:
                for copy in copies[:total] if job == 0 else copies[total:]:
                    wait_all(copy)
            if job == 0:
                wait_all(e_copies)
            for j in range(total):
                lhs = t_ref[half * width : (half + 1) * width, :]
                term = dot(lhs, held[at + j], 1, 0)
                if job < len(extras):
                    term = term + e_held[job, j].astype(F32)
                out_held[at + j] = term.astype(BF16)
            outs += read_in([out_held.at[pl.ds(at, total)]], [o_refs[job]], o_sems.at[pl.ds(job, 1)])
            at += total
        wait_all(outs)

    return pl.pallas_call(
        body,
        in_specs=[ANY] * (1 + parts + len(extras)),
        out_specs=[ANY] * len(jobs),
        out_shape=shapes,
        scratch_shapes=[
            pltpu.VMEM((both, count), BF16),
            pltpu.VMEM((chunks, count, chunk), BF16),
            pltpu.VMEM((chunks, width, chunk), BF16),
            pltpu.VMEM((max(len(extras), 1), 4, width, chunk), BF16),
            pltpu.SemaphoreType.DMA,
            pltpu.SemaphoreType.DMA((chunks, parts)),
            pltpu.SemaphoreType.DMA((len(jobs),)),
            pltpu.SemaphoreType.DMA((max(len(extras), 1),)),
        ],
        compiler_params=params(),
        cost_estimate=cost(2 * chunks * width * count * chunk, chunks * 3 << 18),
        name=name,
    )(grads_t, *rows, *extras)


def row_blocks(pairs, weights, steps, name):
    tile = 512
    halves, rows, both = pairs[0].shape
    width = both // 2
    count = len(steps)

    def body(*refs):
        p_in, w_in, o_refs = refs[:2], refs[2:6], refs[6 : 6 + count]
        p_ref, w_ref, o_held, p_sems, w_sems, o_sems = refs[6 + count :]
        p_copies = read_in(p_in, [p_ref.at[:, :, pl.ds(n * both, both)] for n in range(2)], p_sems)
        w_copies = []
        for n, step in enumerate(steps):
            chip = moved(here()[2], step)
            span = pl.ds(pl.multiple_of((2 * chip + here()[3]) * tile, tile), tile)
            sources = [w.at[span] for w in w_in]
            w_copies.append(
                read_in(sources, [w_ref.at[n, :, pl.ds(m * width, width)] for m in range(4)], w_sems.at[n])
            )
        wait_all(p_copies)
        outs = []
        for n in range(count):
            if n < 2:
                for copy in w_copies[:1] if n == 0 else w_copies[1:]:
                    wait_all(copy)
            for h in range(halves):
                o_held[n, h] = dot(p_ref[h], w_ref[n], 1, 1).astype(BF16)
            outs += read_in([o_held.at[n]], [o_refs[n]], o_sems.at[pl.ds(n, 1)])
        wait_all(outs)

    return pl.pallas_call(
        body,
        in_specs=[ANY] * 6,
        out_specs=[ANY] * count,
        out_shape=[jax.ShapeDtypeStruct((halves, rows, tile), BF16)] * count,
        scratch_shapes=[
            pltpu.VMEM((halves, rows, 2 * both), BF16),
            pltpu.VMEM((count, tile, 2 * both), BF16),
            pltpu.VMEM((count, halves, rows, tile), BF16),
            pltpu.SemaphoreType.DMA((2,)),
            pltpu.SemaphoreType.DMA((count, 4)),
            pltpu.SemaphoreType.DMA((count,)),
        ],
        compiler_params=params(),
        cost_estimate=cost(4 * count * halves * rows * tile * both, (2 + 2 * count) << 20),
        name=name,
    )(*pairs, *weights)


def turn(value, axis, sign):
    def to(i):
        z, x, y, core = i // 32, i // 8 % 4, i // 2 % 4, i % 2
        step = sign * (1 - 2 * core)
        if axis == "z":
            z = (z + step) % 4
        elif axis == "x":
            x = (x + step) % 4
        else:
            y = (y + step) % 4
        return ((z * 4 + x) * 4 + y) * 2 + core

    return lax.ppermute(value, ("seq", "tensor"), [(i, to(i)) for i in range(128)])


def jump(value, axis):
    to = lambda i: i ^ 8 if axis == "z" else i ^ 2
    return lax.ppermute(value, "seq", [(i, to(i)) for i in range(16)])


def swap(value):
    return lax.ppermute(value, "tensor", [(i, i ^ 1) for i in range(8)])


def after(value, *deps):
    return lax.optimization_barrier((value,) + deps)[0]


def ring_sums(own, first, second, name):
    _, width, chunk = own[0].shape

    def body(*refs):
        for n in range(2):
            ins, outs = refs[3 * n : 3 * n + 3], refs[6 + 4 * n : 10 + 4 * n]
            for j in range(4):
                value = sum(r[j].astype(F32) for r in ins)
                outs[j][...] = value if j == 3 else value.astype(BF16)

    whole = VMEM
    shapes = [jax.ShapeDtypeStruct((1, width, chunk), BF16)] * 3 + [jax.ShapeDtypeStruct((1, width, chunk), F32)]
    return pl.pallas_call(
        lambda *refs: body(*refs[:6], *[r.at[0] for r in refs[6:]]),
        in_specs=[whole] * 6,
        out_specs=[whole] * 8,
        out_shape=shapes * 2,
        compiler_params=params(),
        cost_estimate=cost(0, 10 << 20),
        name=name,
    )(own[0], first[0], second[0], own[1], first[1], second[1])


def gather_rows(own, last):
    near = turn(own, "y", 1)
    away = turn(own, "y", -1)
    far = turn(near, "y", 1)
    other = after(far, *last) if last else far
    return [own, swap(own), near, swap(near), away, swap(away), far, swap(other)], near


def local(queries, out_grad, neighbours, key_weight, value_weight, owner, slot, lengths):
    seq_count = lax.axis_size("seq")
    position = lax.axis_index("seq")
    core = here()[3]
    slot_count = lengths.shape[1]
    width = key_weight.shape[1]
    holders = owner.reshape(seq_count, -1)
    slots = slot.reshape(seq_count, -1)
    refs = holders.shape[1]
    order = jnp.arange(refs, dtype=jnp.int32)
    readers = jnp.arange(seq_count, dtype=jnp.int32)

    mine = holders == position
    send_slot = jnp.sum(jnp.where(mine, slots, 0), axis=1)
    my_holder = lax.dynamic_index_in_dim(holders, position, 0, keepdims=False)
    my_slot = lax.dynamic_index_in_dim(slots, position, 0, keepdims=False)
    my_lengths = jnp.take(lengths.reshape(-1), my_holder * slot_count + my_slot, mode="clip")
    back_ref = jnp.sum(jnp.where(my_holder[:, None] == readers[None, :], order[:, None], 0), axis=0)
    reads = mine[:, :, None] & (slots[:, :, None] == jnp.arange(slot_count, dtype=jnp.int32))
    slot_reader = jnp.sum(jnp.where(reads, readers[:, None, None], 0), axis=(0, 1))
    slot_live = jnp.any(reads, axis=(0, 1)).astype(jnp.int32)

    by_slot = neighbours.reshape(slot_count, NT, width)
    got_a = lax.all_to_all(spread(by_slot, send_slot, 0), "seq", split_axis=0, concat_axis=0, tiled=True)
    other_weights = [swap(key_weight), swap(value_weight)]
    send_b = after(spread(by_slot, send_slot, 1), got_a)
    got_b = lax.all_to_all(send_b, "seq", split_axis=0, concat_axis=0, tiled=True)
    rows_a, near_a = gather_rows(pick(got_a, my_holder), ())
    pair_a, all_a = project(rows_a, key_weight, value_weight)
    rows_b, _ = gather_rows(pick(after(got_b, near_a, my_lengths, *other_weights), my_holder), (pair_a,))
    all_b, query_grad, pair, pair_t = project_attend(
        rows_b, key_weight, value_weight, queries, out_grad, pair_a, my_lengths
    )

    def rows_of(earlier, steps, name):
        pairs = [after(pair, *earlier), other_pair] if earlier else [pair, other_pair]
        return row_blocks(pairs, [key_weight, value_weight] + other_weights, steps, name)

    other_pair = swap(pair)
    rows = [all_a, all_b]
    kf, vf, kn, vn = weight_groups(
        pair_t, rows, [(kind, step) for step in (FAR, BACK) for kind in (0, 1)], [], "weight_far"
    )
    (t2,) = rows_of((kf,), [FAR], "row_far")
    far_x, far_z = turn(after(kf, t2), "x", 1), turn(after(vf, t2), "z", 1)
    far_y = turn(t2, "y", 1)
    tn, tm, t0 = rows_of((t2,), [BACK, ON, OWN], "row_next")
    back_y = turn(tn, "y", -1)
    (tm,) = add_into([after(tm, tn)], [far_y])
    onward_y = turn(tm, "y", 1)
    back = [turn(after(kn, far_x, tm), "x", -1), turn(after(vn, far_z, tm), "z", -1)]
    km, vm, ko, vo = weight_groups(
        after(pair_t, tm),
        rows,
        [(kind, step) for step in (ON, OWN) for kind in (0, 1)],
        [far_x, far_z],
        "weight_rest",
    )
    km = after(km, back_y)
    km, vm = after(km, *back), after(vm, *back)
    onward = [turn(km, "x", 1), turn(vm, "z", 1)]

    kf, kn, km, k0, vf, vn, vm, v0 = ring_sums([ko, vo], back, onward, "ring_sums")
    came = [
        [jump(far, axis), turn(behind, axis, -1), turn(ahead, axis, 1)]
        for axis, far, behind, ahead in (("z", kf, kn, km), ("x", vf, vn, vm))
    ]

    returning = sum_and_spread([t0, back_y, onward_y], back_ref)
    arrived = lax.all_to_all(returning, "seq", split_axis=0, concat_axis=0, tiled=True)
    neighbour_grad = settle(arrived, slot_reader, slot_live)

    done = [
        (mine + sum(v.astype(F32) for v in others))[0].T for mine, others in zip((k0, v0), came)
    ]
    return (query_grad, done[0], done[1], neighbour_grad)


def solution(mesh):
    placed = (
        P("seq", "tensor"),
        P("seq", "tensor"),
        P("seq", "tensor"),
        P(None, "tensor"),
        P(None, "tensor"),
        P(),
        P(),
        P(),
    )
    return jax.shard_map(
        local,
        mesh=mesh,
        in_specs=placed,
        out_specs=(P("seq", "tensor"), P("seq", "tensor"), P("seq", "tensor"), P("seq", "tensor")),
        check_vma=False,
    )
```
